32 devices in a mesh: shard: 16 (over z, y, x), replica: 2 (over core).
Axes of the slice: x: 2, y: 2, z: 4, core: 2. Of those that a mesh axis runs over, the one named last changes fastest.
Arguments:
- tokens: bfloat16 [8192, 2048], P(('shard', 'replica')), may hold values from -6 to 6
- seq_lengths: int32 [32, 8], P(('shard', 'replica')), may hold values from 0 to 256, as said below
- in_gain: float32 [2048], replicated, may hold values from 0.5 to 1.5
- q_gain: float32 [128], replicated, may hold values from 0.5 to 1.5
- key_norm_gain: float32 [128], replicated, may hold values from 0.5 to 1.5
- post_gain: float32 [2048], replicated, may hold values from 0.5 to 1.5
- w_qkv: bfloat16 [2048, 4096], P('shard'), may hold values from -0.125 to 0.125
- w_out: bfloat16 [2048, 2048], P('shard'), may hold values from -0.5 to 0.5
- w_gate_up: bfloat16 [2048, 12288], P('shard'), may hold values from -0.125 to 0.125
- w_down: bfloat16 [6144, 2048], P('shard'), may hold values from -0.078125 to 0.078125
- cotangent: bfloat16 [8192, 2048], P(('shard', 'replica')), may hold values from -6 to 6
Outputs:
- result: bfloat16 [8192, 2048], P(('shard', 'replica'))
- grad_tokens: bfloat16 [8192, 2048], P(('shard', 'replica'))
- grad_in_gain: float32 [2048], replicated
- grad_q_gain: float32 [128], replicated
- grad_k_gain: float32 [128], replicated
- grad_post_gain: float32 [2048], replicated
- grad_w_qkv: float32 [2048, 4096], P('shard')
- grad_w_out: float32 [2048, 2048], P('shard')
- grad_w_gate_up: float32 [2048, 12288], P('shard')
- grad_w_down: float32 [6144, 2048], P('shard')
The draws below stay inside these ranges and needn't reach their ends.
Inputs may be any that keep to these rules, and one draw needn't show every extreme that they name: `seq_lengths`: each row lists the lengths of the sequences laid from the start of one pack; zero entries are empty. A row sums to 128 to 256, and some pack holds a single sequence of 256 tokens.
All inputs are finite; a program needn't handle non-finite values.
Results may differ from the reference program's by a relative error of at most 0.014.
Values may be sent and summed in bfloat16 or wider, within the bound.
No kernel may reach another device: no remote copies, remote signals or barrier semaphores. Data moves between devices by JAX's collectives and lax.ppermute only.
A program may use at most 512 MiB of HBM per device.

```python
import math
import jax
import jax.numpy as jnp
from jax import lax

D = 2048
QUERY_HEADS = 16
KEY_VALUE_HEADS = 8
HEAD_SIZE = 128
FF = 6144
PACK_CAPACITY = 256
NSEQ = 8
PACKS = 32
TOKENS = 8192
QKV = 4096


def draw_seq_lengths(key, part):
    key = jax.random.fold_in(key, 11)
    key_count, key_full, key_cut = jax.random.split(key, 3)
    counts = jax.random.randint(key_count, (PACKS,), PACK_CAPACITY // 2, PACK_CAPACITY + 1)
    fullest = jax.random.randint(key_full, (), 0, PACKS)
    rows = jnp.arange(PACKS)
    counts = jnp.where(rows == fullest, PACK_CAPACITY, counts)
    cuts = jax.random.randint(key_cut, (PACKS, NSEQ - 1), 0, PACK_CAPACITY + 1)
    cuts = jnp.where((rows == fullest)[:, None], PACK_CAPACITY, jnp.minimum(cuts, counts[:, None]))
    cuts = jnp.sort(cuts, axis=1)
    bounds = jnp.concatenate([jnp.zeros((PACKS, 1), jnp.int32), cuts.astype(jnp.int32), counts[:, None].astype(jnp.int32)], axis=1)
    return (bounds[:, 1:] - bounds[:, :-1]).astype(jnp.int32)


def block_levels(rng, shape, cuts, low, top_value):
    def one(axis_at, blocks):
        steps = jax.random.uniform(jax.random.fold_in(jax.random.fold_in(rng, 6), axis_at), (blocks,), jnp.float32, low / len(cuts), top_value / len(cuts))
        return jnp.repeat(jnp.exp(steps), shape[axis_at] // blocks).reshape((-1,) + (1,) * (len(shape) - axis_at - 1))

    level = one(*cuts[0])
    for cut in cuts[1:]:
        level = level * one(*cut)
    return level


def gaussian(rng, extent, width, reach, cuts=(), held_as=jnp.bfloat16):
    drawn = width * jax.random.normal(rng, extent, jnp.float32)
    if cuts:
        drawn = drawn * block_levels(rng, extent, cuts, -0.22, 0.18)
    return jnp.clip(drawn, -reach, reach).astype(held_as)


def setup_inputs(seed: int = 0) -> dict:
    key_of = jax.random.split(jax.random.key(seed), 12)
    tokens = gaussian(key_of[0], (TOKENS, D), 1.0, 6.0, ((0, 32),))
    seq_lengths = draw_seq_lengths(jax.random.fold_in(key_of[11], 71), 0)
    in_gain = jnp.clip(1.0 + 0.1 * jax.random.normal(key_of[2], (D,), jnp.float32), 0.5, 1.5)
    q_gain = jnp.clip(1.0 + 0.1 * jax.random.normal(key_of[3], (HEAD_SIZE,), jnp.float32), 0.5, 1.5)
    key_norm_gain = jnp.clip(1.0 + 0.1 * jax.random.normal(key_of[4], (HEAD_SIZE,), jnp.float32), 0.5, 1.5)
    post_gain = jnp.clip(1.0 + 0.1 * jax.random.normal(key_of[5], (D,), jnp.float32), 0.5, 1.5)
    w_qkv = gaussian(key_of[6], (D, QKV), D ** -0.5, 0.125, ((0, 16),))
    w_out = gaussian(key_of[7], (QUERY_HEADS * HEAD_SIZE, D), (QUERY_HEADS * HEAD_SIZE // 16) ** -0.5, 0.5, ((0, 16),))
    w_gate_up = gaussian(key_of[8], (D, 2 * FF), D ** -0.5, 0.125, ((0, 16),))
    w_down = gaussian(key_of[9], (FF, D), FF ** -0.5, 0.078125, ((0, 16),))
    cotangent = gaussian(key_of[10], (TOKENS, D), 1.0, 6.0, ((0, 32),))
    return {"tokens": tokens, "seq_lengths": seq_lengths, "in_gain": in_gain, "q_gain": q_gain, "key_norm_gain": key_norm_gain, "post_gain": post_gain, "w_qkv": w_qkv, "w_out": w_out, "w_gate_up": w_gate_up, "w_down": w_down, "cotangent": cotangent}


EPS = 1e-06
ROPE_BASE = 1000000.0
MASKED = -1e+30
HIGHEST = lax.Precision.HIGHEST

@jax.custom_vjp
def low(v):
    return lax.optimization_barrier(v.astype(jnp.bfloat16)).astype(jnp.float32)

@jax.custom_vjp
def low_back(v):
    return v

def low_keep(v):
    return (low(v), None)

def low_pass(kept, grad):
    return (grad,)

def back_keep(v):
    return (v, None)

def back_low(kept, grad):
    return (low(grad),)
low.defvjp(low_keep, low_pass)
low_back.defvjp(back_keep, back_low)

def pack_layout(lengths):
    ends = jnp.cumsum(lengths).astype(jnp.int32)
    starts = (ends - lengths).astype(jnp.int32)
    slots = jnp.arange(PACK_CAPACITY, dtype=jnp.int32)
    segment = lax.optimization_barrier(jnp.sum((slots[:, None] >= ends[None, :]).astype(jnp.int32), axis=1))
    live = slots < ends[-1]
    labels = jnp.arange(NSEQ, dtype=jnp.int32)
    begin = lax.optimization_barrier(jnp.sum(jnp.where(segment[:, None] == labels[None, :], starts[None, :], 0), axis=1)).astype(jnp.int32)
    position = (slots - begin).astype(jnp.float32)
    segids = jnp.where(live, segment, NSEQ + slots).astype(jnp.int32)
    freqs = ROPE_BASE ** (-2.0 * jnp.arange(HEAD_SIZE // 2, dtype=jnp.float32) / HEAD_SIZE)
    angle = position[:, None] * freqs[None, :]
    cosine = jnp.concatenate([jnp.cos(angle), jnp.cos(angle)], axis=1)
    sine = jnp.concatenate([jnp.sin(angle), jnp.sin(angle)], axis=1)
    return (segids, cosine, sine, live)

def normalized_rows(value, gain):
    return value * lax.rsqrt(lax.optimization_barrier(jnp.mean(value * value, axis=-1, keepdims=True)) + EPS) * gain

def rotate_halves(value, cosine, sine):
    half = HEAD_SIZE // 2
    rotated = jnp.concatenate([-value[..., half:], value[..., :half]], axis=-1)
    return value * cosine + rotated * sine

def group_layer(params, block_rows, block_lengths):
    in_gain, q_gain, key_norm_gain, post_gain, w_qkv, w_out, w_gate_up, w_down = params
    token_packs = block_lengths.shape[0]
    replica_groupings = QUERY_HEADS // KEY_VALUE_HEADS
    segids, cosine, sine, live = jax.vmap(pack_layout)(block_lengths)
    cosine_per_head = cosine[:, :, None, :]
    sine_per_head = sine[:, :, None, :]
    first = low(normalized_rows(block_rows, in_gain))
    attention_mixed = low_back(jnp.dot(first, w_qkv, precision=HIGHEST))
    attention_mixed = attention_mixed.reshape(token_packs, PACK_CAPACITY, QUERY_HEADS + 2 * KEY_VALUE_HEADS, HEAD_SIZE)
    query_rows = low(rotate_halves(normalized_rows(attention_mixed[:, :, :QUERY_HEADS], q_gain), cosine_per_head, sine_per_head))
    key_rows = low(rotate_halves(normalized_rows(attention_mixed[:, :, QUERY_HEADS:QUERY_HEADS + KEY_VALUE_HEADS], key_norm_gain), cosine_per_head, sine_per_head))
    value_rows = low(attention_mixed[:, :, QUERY_HEADS + KEY_VALUE_HEADS:])
    query_rows = query_rows.reshape(token_packs, PACK_CAPACITY, KEY_VALUE_HEADS, replica_groupings, HEAD_SIZE)
    scores = low_back(jnp.einsum('bqgrd,bkgd->bgrqk', query_rows, key_rows, precision=HIGHEST) * (1.0 / math.sqrt(HEAD_SIZE)))
    slots = jnp.arange(PACK_CAPACITY, dtype=jnp.int32)
    allowed = (segids[:, :, None] == segids[:, None, :]) & (slots[:, None] >= slots[None, :])[None]
    scores = jnp.where(allowed[:, None, None], scores, MASKED)
    probs = low(jax.nn.softmax(scores, axis=-1))
    attn = jnp.einsum('bgrqk,bkgd->bqgrd', probs, value_rows, precision=HIGHEST)
    attn = low(low_back(attn.reshape(token_packs * PACK_CAPACITY, QUERY_HEADS * HEAD_SIZE)))
    middle = block_rows + low_back(jnp.dot(attn, w_out, precision=HIGHEST))
    second = low(normalized_rows(middle, post_gain))
    both = low_back(jnp.dot(second, w_gate_up, precision=HIGHEST))
    hidden = low(jax.nn.silu(both[:, :FF]) * both[:, FF:])
    return middle + low_back(jnp.dot(hidden, w_down, precision=HIGHEST))

def reference(tokens, seq_lengths, in_gain, q_gain, key_norm_gain, post_gain, w_qkv, w_out, w_gate_up, w_down, cotangent):
    params = (in_gain.astype(jnp.float32), q_gain.astype(jnp.float32), key_norm_gain.astype(jnp.float32), post_gain.astype(jnp.float32), w_qkv.astype(jnp.float32), w_out.astype(jnp.float32), w_gate_up.astype(jnp.float32), w_down.astype(jnp.float32))
    inputs = tokens.astype(jnp.float32)
    group = math.gcd(PACKS, max(1, 4096 // PACK_CAPACITY))
    blocks = PACKS // group
    lengths = seq_lengths.reshape(blocks, group, NSEQ)
    step_fn = jax.checkpoint(group_layer)

    def whole(params, inputs):
        rows = inputs.reshape(blocks, group * PACK_CAPACITY, D)

        def scan_body(carry, item):
            return (carry, step_fn(params, item[0], item[1]))
        unused, outputs = lax.scan(scan_body, jnp.zeros((), jnp.float32), (rows, lengths))
        return outputs.reshape(TOKENS, D)
    outputs, pull = jax.vjp(whole, params, inputs)
    live = jax.vmap(pack_layout)(seq_lengths)[3].reshape(TOKENS)
    grad_out = cotangent.astype(jnp.float32) * live[:, None].astype(jnp.float32)
    grad_params, grad_inputs = pull(grad_out)
    return (outputs.astype(jnp.bfloat16), grad_inputs.astype(jnp.bfloat16), grad_params[0], grad_params[1], grad_params[2], grad_params[3], grad_params[4], grad_params[5], grad_params[6], grad_params[7])
```

```python
import math

import jax
import jax.numpy as jnp
from jax import lax
from jax.experimental import pallas as pl
from jax.experimental.pallas import tpu as pltpu
from jax.sharding import PartitionSpec as P

QUERY_HEADS = 16
KEY_VALUE_HEADS = 8
HEAD_SIZE = 128
FF = 6144
PACK_CAPACITY = 256
NSEQ = 8
GROUPS = QUERY_HEADS // KEY_VALUE_HEADS


EPS = 1e-06
ROPE_BASE = 1000000.0
MASKED = -1e30
AXES = ("shard", "replica")
F32, BF16 = jnp.float32, jnp.bfloat16
SCALE = 1.0 / math.sqrt(HEAD_SIZE)
VMEM = 60 << 20


def pack_layout(lengths):
    ends = jnp.cumsum(lengths)
    starts = ends - lengths
    slots = jnp.arange(PACK_CAPACITY, dtype=jnp.int32)
    segment = jnp.sum((slots[:, None] >= ends[None, :]).astype(jnp.int32), axis=1)
    live = slots < ends[-1]
    labels = jnp.arange(NSEQ, dtype=jnp.int32)
    begin = jnp.sum(jnp.where(segment[:, None] == labels[None, :], starts[None, :], 0), axis=1)
    position = (slots - begin).astype(jnp.float32)
    segids = jnp.where(live, segment, NSEQ + slots)
    freqs = ROPE_BASE ** (-2.0 * jnp.arange(HEAD_SIZE // 2, dtype=jnp.float32) / HEAD_SIZE)
    angle = position[:, None] * freqs[None, :]
    cosine = jnp.concatenate([jnp.cos(angle), jnp.cos(angle)], axis=1)
    sine = jnp.concatenate([jnp.sin(angle), jnp.sin(angle)], axis=1)
    return (segids, cosine, sine, live)


def normalized_rows(value, gain):
    scale_inv = lax.rsqrt(jnp.mean(value * value, axis=-1, keepdims=True) + EPS)
    normed = value * scale_inv
    return (normed * gain, normed, scale_inv)


def norm_back(grad, normed, scale_inv, gain):
    scaled = grad * gain
    grad_in = scale_inv * (scaled - normed * jnp.mean(scaled * normed, axis=-1, keepdims=True))
    grad_gain = jnp.sum((grad * normed).reshape(-1, normed.shape[-1]), axis=0)
    return (grad_in, grad_gain)


def against(grad, matrix):
    return lax.dot_general(
        grad, matrix, (((1,), (1,)), ((), ())), preferred_element_type=jnp.float32
    )


def through(left, grad):
    return lax.dot_general(left, grad, (((0,), (0,)), ((), ())), preferred_element_type=jnp.float32)


class Wires:
    def __init__(self, shards, copies):
        self.shards, self.copies = shards, copies
        bits = shards.bit_length() - 1
        self.masks = [1 << b for b in range(bits)]
        self.top = shards >> 1
        self.team = [1, 4]
        self.far = [m for m in self.masks if m > 4]
        self.spread = self.far + [2]
        self.me = lax.axis_index("shard")
        self.core = lax.axis_index("replica")

    def send(self, value, to):
        pairs = []
        for i in range(self.shards * self.copies):
            goal = to(i // self.copies, i % self.copies)
            if goal is not None:
                pairs.append((i, goal[0] * self.copies + goal[1]))
        return lax.ppermute(value, AXES, pairs)

    def swap(self, value, mask):
        return self.send(value, lambda s, c: (s ^ mask, c))

    def swap_core(self, value):
        return self.send(value, lambda s, c: (s, 1 - c))

    def has(self, mask):
        return (self.me & mask) != 0

    def place(self, shard):
        at = 0
        for i, mask in enumerate(self.spread):
            at = at + ((shard // mask) % 2) * (1 << i)
        return at

    def others(self):
        team = self.team[0] | self.team[1]
        return sorted((s for s in range(self.shards) if s & team == 0), key=self.place)


def masks_of(order):
    out = [0]
    for mask in reversed(order):
        out = out + [mask ^ m for m in out]
    return out


def pick_columns(value, block, groups):
    rows, width = value.shape
    places = jnp.stack([jnp.asarray(g, jnp.int32) for group in groups for g in group])
    if block % 128:
        blocks = value.reshape(rows, width // block, block)
        out, at = [], 0
        for group in groups:
            taken = jnp.take(blocks, places[at : at + len(group)], axis=1)
            out.append(taken.reshape(rows, len(group) * block))
            at += len(group)
        return out
    tile = math.gcd(rows, 256)

    def kernel(places_ref, in_ref, *out_refs):
        at = 0
        for group, out_ref in zip(groups, out_refs):
            for i in range(len(group)):
                start = pl.multiple_of(places_ref[at] * block, 128)
                out_ref[:, i * block : (i + 1) * block] = in_ref[:, pl.ds(start, block)]
                at += 1

    widths = [len(group) * block for group in groups]
    return list(
        pl.pallas_call(
            kernel,
            grid_spec=pltpu.PrefetchScalarGridSpec(
                num_scalar_prefetch=1,
                grid=(rows // tile,),
                in_specs=[pl.BlockSpec((tile, width), lambda i, s: (i, 0))],
                out_specs=[pl.BlockSpec((tile, w), lambda i, s: (i, 0)) for w in widths],
            ),
            out_shape=[jax.ShapeDtypeStruct((rows, w), value.dtype) for w in widths],
            compiler_params=pltpu.CompilerParams(vmem_limit_bytes=VMEM),
            cost_estimate=pl.CostEstimate(
                flops=0, bytes_accessed=2 * rows * (width + sum(widths)), transcendentals=0
            ),
            name="pick_columns",
        )(places, value)
    )


def put_columns(values, block, groups):
    rows = values[0].shape[0]
    places = jnp.stack([jnp.asarray(g, jnp.int32) for group in groups for g in group])
    width = block * places.shape[0]
    if block % 128:
        flat = jnp.concatenate([v.astype(F32) for v in values], axis=1)
        blocks = flat.reshape(rows, width // block, block)
        return jnp.zeros_like(blocks).at[:, places].set(blocks).reshape(rows, width)
    tile = math.gcd(rows, 32)

    def kernel(places_ref, *refs):
        out_ref, at = refs[-1], 0
        for group, ref in zip(groups, refs[:-1]):
            for i in range(len(group)):
                start = pl.multiple_of(places_ref[at] * block, 128)
                part = ref[:, i * block : (i + 1) * block]
                out_ref[:, pl.ds(start, block)] = part.astype(F32)
                at += 1

    return pl.pallas_call(
        kernel,
        grid_spec=pltpu.PrefetchScalarGridSpec(
            num_scalar_prefetch=1,
            grid=(rows // tile,),
            in_specs=[pl.BlockSpec((tile, v.shape[1]), lambda i, s: (i, 0)) for v in values],
            out_specs=pl.BlockSpec((tile, width), lambda i, s: (i, 0)),
        ),
        out_shape=jax.ShapeDtypeStruct((rows, width), F32),
        compiler_params=pltpu.CompilerParams(vmem_limit_bytes=VMEM),
        cost_estimate=pl.CostEstimate(flops=0, bytes_accessed=7 * rows * width, transcendentals=0),
        name="put_columns",
    )(places, *values)


def collect(wires, own, order):
    pieces = [own]
    for at, mask in enumerate(order):
        if at == 2:
            pieces = [jnp.concatenate(pieces, axis=0)]
        pieces = pieces + [wires.swap(p, mask) for p in pieces]
    return pieces


def collect_in_order(wires, own, order):
    for mask in order:
        got, bit = wires.swap(own, mask), wires.has(mask)
        own = jnp.concatenate([jnp.where(bit, got, own), jnp.where(bit, own, got)], axis=0)
    return own


def scatter_sum(wires, keep, order):
    for mask in order:
        half = keep.shape[0] // 2
        got = wires.swap(keep[half:].astype(BF16), mask)
        keep = keep[:half].astype(F32) + got.astype(F32)
    return keep


def gather_team(wires, value):
    one, two = wires.team
    by_two = wires.swap(value, two)
    by_one = wires.swap(value, one)
    return [value, by_one, by_two, wires.swap(by_two, one)]


def sum_team(wires, parts):
    one, two = wires.team
    got_two = wires.swap(parts[3].astype(BF16), one)
    got_own = wires.swap(parts[1].astype(BF16), one)
    for_two = parts[2].astype(F32) + got_two.astype(F32)
    got = wires.swap(for_two.astype(BF16), two)
    return parts[0].astype(F32) + got_own.astype(F32) + got.astype(F32)


def team_blocks(wires, half):
    one, two = wires.team
    mine = wires.me & (one | two)
    return [
        [half * wires.shards + ((mine ^ t) | s) for s in wires.others()]
        for t in (0, one, two, one | two)
    ]


def turned(value):
    return pltpu.roll(value, HEAD_SIZE // 2, 1)


def head_forward(raw, gain, cosine, sine):
    scale = lax.rsqrt(jnp.mean(raw * raw, axis=1, keepdims=True) + EPS)
    normed = raw * scale
    v = normed * gain
    return (v * cosine + turned(v) * sine).astype(BF16), normed, scale


def head_back(grad, normed, scale, gain, cosine, sine):
    g = grad * cosine + turned(grad * sine)
    scaled = g * gain
    raw = scale * (scaled - normed * jnp.mean(scaled * normed, axis=1, keepdims=True))
    return raw, jnp.sum(g * normed, axis=0, keepdims=True)


def attend_group(first, pieces, cosine, sine, bias, q_gain, k_gain):
    tokens = first.shape[0]
    packs = tokens // PACK_CAPACITY
    width = (GROUPS + 2) * HEAD_SIZE
    n = len(pieces)
    depth = first.shape[1] // n

    def kernel(first_ref, *refs):
        w_refs = refs[:n]
        cos_ref, sin_ref, bias_ref, qg_ref, kg_ref, attn_ref, mixed_ref = refs[n:]
        mixed = jnp.zeros((tokens, width), F32)
        for i in range(n):
            mixed += jnp.dot(
                first_ref[:, i * depth : (i + 1) * depth], w_refs[i][...],
                preferred_element_type=F32,
            )
        mixed_ref[...] = mixed
        for p in range(packs):
            at = slice(p * PACK_CAPACITY, (p + 1) * PACK_CAPACITY)
            cosine, sine, bias = cos_ref[at], sin_ref[at], bias_ref[at]
            head = lambda j: mixed_ref[at, j * HEAD_SIZE : (j + 1) * HEAD_SIZE]
            key, _, _ = head_forward(head(GROUPS), kg_ref[...], cosine, sine)
            value = head(GROUPS + 1).astype(BF16)
            for j in range(GROUPS):
                query, _, _ = head_forward(head(j), qg_ref[...], cosine, sine)
                scores = against(query, key) * SCALE + bias
                expd = jnp.exp(scores - jnp.max(scores, axis=1, keepdims=True))
                probs = expd / jnp.sum(expd, axis=1, keepdims=True)
                attn = jnp.dot(probs.astype(BF16), value, preferred_element_type=F32)
                attn_ref[at, j * HEAD_SIZE : (j + 1) * HEAD_SIZE] = attn.astype(BF16)

    return pl.pallas_call(
        kernel,
        out_shape=[
            jax.ShapeDtypeStruct((tokens, GROUPS * HEAD_SIZE), BF16),
            jax.ShapeDtypeStruct((tokens, width), F32),
        ],
        compiler_params=pltpu.CompilerParams(vmem_limit_bytes=VMEM),
        cost_estimate=pl.CostEstimate(
            flops=2 * tokens * first.shape[1] * width + 8 * tokens * PACK_CAPACITY * HEAD_SIZE,
            bytes_accessed=2 * first.size + 2 * first.shape[1] * width + 6 * tokens * width,
            transcendentals=GROUPS * tokens * PACK_CAPACITY,
        ),
        name="attend_group",
    )(first, *pieces, cosine, sine, bias, q_gain, k_gain)


def attend_group_back(mixed, grad, cosine, sine, bias, q_gain, k_gain):
    tokens, width = mixed.shape
    packs = tokens // PACK_CAPACITY

    def kernel(mixed_ref, grad_ref, cos_ref, sin_ref, bias_ref, qg_ref, kg_ref, out_ref, gain_ref):
        q_gain, k_gain = qg_ref[...], kg_ref[...]
        q_sum = jnp.zeros((1, HEAD_SIZE), F32)
        k_sum = jnp.zeros((1, HEAD_SIZE), F32)
        for p in range(packs):
            at = slice(p * PACK_CAPACITY, (p + 1) * PACK_CAPACITY)
            cosine, sine, bias = cos_ref[at], sin_ref[at], bias_ref[at]
            head = lambda j: mixed_ref[at, j * HEAD_SIZE : (j + 1) * HEAD_SIZE]
            key, key_normed, key_scale = head_forward(head(GROUPS), k_gain, cosine, sine)
            value = head(GROUPS + 1).astype(BF16)
            grad_key = jnp.zeros((PACK_CAPACITY, HEAD_SIZE), F32)
            grad_value = jnp.zeros((PACK_CAPACITY, HEAD_SIZE), F32)
            for j in range(GROUPS):
                cols = slice(j * HEAD_SIZE, (j + 1) * HEAD_SIZE)
                query, normed, scale = head_forward(head(j), q_gain, cosine, sine)
                g = grad_ref[at, cols]
                scores = against(query, key) * SCALE + bias
                expd = jnp.exp(scores - jnp.max(scores, axis=1, keepdims=True))
                probs = expd / jnp.sum(expd, axis=1, keepdims=True)
                dprobs = against(g, value)
                inner = jnp.sum(probs * dprobs, axis=1, keepdims=True)
                grad_scores = (probs * (dprobs - inner)).astype(BF16)
                grad_query = jnp.dot(grad_scores, key, preferred_element_type=F32) * SCALE
                grad_key += through(grad_scores, query)
                grad_value += through(probs.astype(BF16), g)
                raw, gain = head_back(grad_query, normed, scale, q_gain, cosine, sine)
                out_ref[at, cols] = raw.astype(BF16)
                q_sum += gain
            raw, gain = head_back(grad_key * SCALE, key_normed, key_scale, k_gain, cosine, sine)
            k_sum += gain
            out_ref[at, GROUPS * HEAD_SIZE : (GROUPS + 1) * HEAD_SIZE] = raw.astype(BF16)
            out_ref[at, (GROUPS + 1) * HEAD_SIZE :] = grad_value.astype(BF16)
        gain_ref[...] = jnp.concatenate([q_sum, k_sum] + [jnp.zeros_like(q_sum)] * 6, axis=0)

    return pl.pallas_call(
        kernel,
        out_shape=[
            jax.ShapeDtypeStruct((tokens, width), BF16),
            jax.ShapeDtypeStruct((8, HEAD_SIZE), F32),
        ],
        compiler_params=pltpu.CompilerParams(vmem_limit_bytes=VMEM),
        cost_estimate=pl.CostEstimate(
            flops=20 * tokens * PACK_CAPACITY * HEAD_SIZE,
            bytes_accessed=8 * tokens * width,
            transcendentals=GROUPS * tokens * PACK_CAPACITY,
        ),
        name="attend_group_back",
    )(mixed, grad, cosine, sine, bias, q_gain, k_gain)


def spread_back(grads, weights, groups, block):
    tokens = grads[0].shape[0]
    width = sum(w.shape[0] for w in weights[0])
    places = jnp.stack([jnp.asarray(g, jnp.int32) for group in groups for g in group])
    if block % 128:
        total = 0.0
        for grad, pieces, group in zip(grads, weights, groups):
            part = jnp.concatenate([against(grad, w) for w in pieces], axis=1)
            total = total + put_columns([part], block, [group])
        return total
    flat = [w for pieces in weights for w in pieces]

    def kernel(places_ref, *refs):
        grad_refs, refs = refs[: len(grads)], refs[len(grads) :]
        out_ref, at, k = refs[-1], 0, 0
        for gi, grad_ref in enumerate(grad_refs):
            for _ in weights[gi]:
                part = against(grad_ref[...], refs[k][...])
                for b in range(part.shape[1] // block):
                    start = pl.multiple_of(places_ref[at] * block, 128)
                    cols = pl.ds(start, block)
                    new = part[:, b * block : (b + 1) * block]
                    out_ref[:, cols] = new if gi == 0 else out_ref[:, cols] + new
                    at += 1
                k += 1

    whole = lambda v: pl.BlockSpec(v.shape, lambda i, s: (0, 0))
    return pl.pallas_call(
        kernel,
        grid_spec=pltpu.PrefetchScalarGridSpec(
            num_scalar_prefetch=1,
            grid=(1,),
            in_specs=[whole(v) for v in grads] + [whole(w) for w in flat],
            out_specs=pl.BlockSpec((tokens, width), lambda i, s: (0, 0)),
        ),
        out_shape=jax.ShapeDtypeStruct((tokens, width), F32),
        compiler_params=pltpu.CompilerParams(vmem_limit_bytes=VMEM),
        cost_estimate=pl.CostEstimate(
            flops=2 * tokens * sum(w.size for w in flat),
            bytes_accessed=2 * sum(w.size for w in flat) + 8 * tokens * width,
            transcendentals=0,
        ),
        name="spread_back",
    )(places, *grads, *flat)


def feed_forward(second, own, other, grad_low, down_own, down_other, core):
    tokens, d = second.shape
    units = down_own.shape[0]
    n = len(own)
    depth = d // n
    tile, rows = 384, 256

    def kernel(core_ref, x_ref, go_ref, gx_ref, *refs):
        own_refs, other_refs = refs[:n], refs[n : 2 * n]
        do_ref, dx_ref, hidden_ref, out_own_ref, out_other_ref = refs[2 * n :]
        first = core_ref[0] == 0

        @pl.loop(0, tokens // rows)
        def _(r):
            at = pl.ds(pl.multiple_of(r * rows, rows), rows)
            a = jnp.zeros((rows, tile), F32)
            b = jnp.zeros((rows, tile), F32)
            for i in range(n):
                x = x_ref[at, i * depth : (i + 1) * depth]
                a += jnp.dot(x, own_refs[i][...], preferred_element_type=F32)
                b += jnp.dot(x, other_refs[i][...], preferred_element_type=F32)
            gate, upward = jnp.where(first, a, b), jnp.where(first, b, a)
            sigma = jax.nn.sigmoid(gate)
            silu = gate * sigma
            hidden_ref[at, :] = (silu * upward).astype(BF16)
            grad = against(go_ref[at, :], do_ref[...]) + against(gx_ref[at, :], dx_ref[...])
            grad_gate = grad * upward * sigma * (1.0 + gate * (1.0 - sigma))
            grad_up = grad * silu
            out_own_ref[at, :] = jnp.where(first, grad_gate, grad_up).astype(BF16)
            out_other_ref[at, :] = jnp.where(first, grad_up, grad_gate).astype(BF16)

    once = pl.Buffered(1)
    half = d // 2
    in_specs = [
        pl.BlockSpec((tokens, d), lambda j, s: (0, 0), pipeline_mode=once),
        pl.BlockSpec((tokens, half), lambda j, s: (0, s[0]), pipeline_mode=once),
        pl.BlockSpec((tokens, half), lambda j, s: (0, 1 - s[0]), pipeline_mode=once),
    ]
    in_specs += [pl.BlockSpec((depth, tile), lambda j, s: (0, j))] * (2 * n)
    in_specs += [pl.BlockSpec((tile, half), lambda j, s: (j, 0))] * 2
    return pl.pallas_call(
        kernel,
        grid_spec=pltpu.PrefetchScalarGridSpec(
            num_scalar_prefetch=1,
            grid=(units // tile,),
            in_specs=in_specs,
            out_specs=[pl.BlockSpec((tokens, tile), lambda j, s: (0, j))] * 3,
        ),
        out_shape=[jax.ShapeDtypeStruct((tokens, units), BF16)] * 3,
        compiler_params=pltpu.CompilerParams(vmem_limit_bytes=VMEM),
        cost_estimate=pl.CostEstimate(
            flops=6 * tokens * d * units,
            bytes_accessed=4 * tokens * d + 6 * d * units + 6 * tokens * units,
            transcendentals=tokens * units,
        ),
        name="feed_forward",
    )(core.reshape(1), second, grad_low, grad_low, *own, *other, down_own, down_other)


def feed_forward_back(grad_own, grad_other, own, other, places, block):
    tokens, units = grad_own.shape
    d = sum(w.shape[0] for w in own)
    if block % 128:
        parts = [against(grad_own, a) + against(grad_other, b) for a, b in zip(own, other)]
        return put_columns([jnp.concatenate(parts, axis=1)], block, [places]).astype(BF16)
    n, rows = len(own), 256

    def kernel(places_ref, go_ref, gx_ref, *refs):
        own_refs, other_refs, out_ref = refs[:n], refs[n : 2 * n], refs[2 * n]
        at = 0
        for i in range(n):
            part = against(go_ref[...], own_refs[i][...])
            part += against(gx_ref[...], other_refs[i][...])
            for b in range(part.shape[1] // block):
                start = pl.multiple_of(places_ref[at] * block, 128)
                out_ref[:, pl.ds(start, block)] = part[:, b * block : (b + 1) * block].astype(BF16)
                at += 1

    return pl.pallas_call(
        kernel,
        grid_spec=pltpu.PrefetchScalarGridSpec(
            num_scalar_prefetch=1,
            grid=(tokens // rows,),
            in_specs=[pl.BlockSpec((rows, units), lambda i, s: (i, 0))] * 2
            + [
                pl.BlockSpec(w.shape, lambda i, s: (0, 0), pipeline_mode=pl.Buffered(1))
                for w in own + other
            ],
            out_specs=pl.BlockSpec((rows, d), lambda i, s: (i, 0)),
        ),
        out_shape=jax.ShapeDtypeStruct((tokens, d), BF16),
        compiler_params=pltpu.CompilerParams(vmem_limit_bytes=VMEM),
        cost_estimate=pl.CostEstimate(
            flops=4 * tokens * d * units,
            bytes_accessed=4 * d * units + 4 * tokens * units + 2 * tokens * d,
            transcendentals=0,
        ),
        name="feed_forward_back",
    )(jnp.stack([jnp.asarray(p, jnp.int32) for p in places]), grad_own, grad_other, *own, *other)


def tables(lengths):
    segids, cosine, sine, live = pack_layout(lengths)
    slots = jnp.arange(PACK_CAPACITY, dtype=jnp.int32)
    allowed = (segids[:, None] == segids[None, :]) & (slots[:, None] >= slots[None, :])
    half = HEAD_SIZE // 2
    sine = jnp.concatenate([-sine[:, :half], sine[:, half:]], axis=1)
    return cosine, sine, jnp.where(allowed, 0.0, MASKED).astype(F32), live


def on_device(
    shards,
    copies,
    tokens,
    seq_lengths,
    in_gain,
    q_gain,
    key_norm_gain,
    post_gain,
    w_qkv,
    w_out,
    w_gate_up,
    w_down,
    cotangent,
):
    wires = Wires(shards, copies)
    me, core, top = wires.me, wires.core, wires.top
    first_core = core == 0
    rows = w_qkv.shape[0]
    d = in_gain.shape[0]
    half = d // 2
    by_core = lambda own, other: (jnp.where(first_core, own, other), jnp.where(first_core, other, own))
    ordered = lambda own, other: jnp.concatenate(by_core(own, other), axis=-1)
    dot = lambda a, b: jnp.dot(a, b, preferred_element_type=F32)
    through_low = lambda a, b: through(a, b).astype(BF16)
    both_packs = lambda v: jnp.concatenate([v, wires.swap_core(v)], axis=0)

    per_core = KEY_VALUE_HEADS // 2
    column_groups = [
        [GROUPS * (per_core * core + g) + j for j in range(GROUPS)]
        + [QUERY_HEADS + per_core * core + g, QUERY_HEADS + KEY_VALUE_HEADS + per_core * core + g]
        for g in range(per_core)
    ]
    orders = [wires.far + o for o in ([1, 2, 4], [2, 4, 1], [4, 1, 2], [1, 4, 2])]
    qkv = [
        collect(wires, half_group, order)
        for half_group, order in zip(pick_columns(w_qkv, HEAD_SIZE, column_groups), orders)
    ]
    at_home = wires.has(top) == (core == 1)
    away = wires.send(w_out, lambda s, c: (s ^ top, c) if (s & top != 0) == (c == 1) else None)
    out_order = [m for m in wires.far if m != top] + [1, 2, 4]
    out_pieces = collect(wires, jnp.where(at_home, w_out, away), out_order)
    out_back = out_order[::-1]
    out_rel = masks_of(out_back)

    inputs = tokens.astype(F32)
    first, first_normed, first_scale = normalized_rows(inputs, in_gain)
    first_low = both_packs(first.astype(BF16))
    block_places = [[me ^ m for m in masks_of(order[::-1])] for order in orders]
    first_moved = pick_columns(first_low, rows, block_places)
    lengths = seq_lengths.astype(F32)
    lengths_other = wires.swap_core(lengths)[0].astype(jnp.int32)
    cosine, sine, bias, live = tables(seq_lengths[0])
    packs = [
        jnp.concatenate(pair, axis=0)
        for pair in zip((cosine, sine, bias), tables(lengths_other)[:3])
    ]
    gains = [q_gain.reshape(1, -1), key_norm_gain.reshape(1, -1)]
    attn, mixed = zip(
        *[attend_group(x, w, *packs, *gains) for x, w in zip(first_moved, qkv)]
    )
    below = top - 1
    (attn_moved,) = pick_columns(
        jnp.concatenate(attn, axis=1), rows, [[(me & below) ^ m for m in out_rel]]
    )
    depth = attn_moved.shape[1] // len(out_pieces)
    out_part = sum(
        dot(attn_moved[:, i * depth : (i + 1) * depth], w) for i, w in enumerate(out_pieces)
    )
    out_got = wires.swap_core(out_part[PACK_CAPACITY:].astype(BF16))
    middle = inputs + (out_part[:PACK_CAPACITY] + out_got.astype(F32))
    second, second_normed, second_scale = normalized_rows(middle, post_gain)

    one, two = wires.team
    team = [0, one, two, one | two]
    gu_parts = pick_columns(w_gate_up, FF // shards, team_blocks(wires, core))
    gu_got = [gu_parts[0]] + [wires.swap(p, t) for p, t in zip(gu_parts[1:], team[1:])]
    gu_own = collect(wires, jnp.concatenate(gu_got, axis=0), wires.spread)
    gu_other = [wires.swap_core(p) for p in gu_own]
    (down_half,) = pick_columns(w_down, half, [[core]])
    down_own = collect_in_order(wires, down_half, wires.spread)
    down_other = wires.swap_core(down_own)

    grad_out = cotangent.astype(F32) * live[:, None].astype(F32)
    grad_low_team = jnp.concatenate(gather_team(wires, grad_out.astype(BF16)), axis=0)

    second_team = jnp.concatenate(gather_team(wires, second.astype(BF16)), axis=0)
    back = wires.spread[::-1]
    row_places = [me ^ m for m in masks_of(back + [two, one])]
    (second_moved,) = pick_columns(second_team, rows, [row_places])
    hidden_low, grad_own, grad_other = feed_forward(
        second_moved, gu_own, gu_other, grad_low_team, down_own, down_other, core
    )
    split = lambda v: [v[i * PACK_CAPACITY : (i + 1) * PACK_CAPACITY] for i in range(4)]
    grad_second = sum_team(
        wires, split(feed_forward_back(grad_own, grad_other, gu_own, gu_other, row_places, rows))
    )
    partial = jnp.concatenate([dot(hidden_low, down_own), dot(hidden_low, down_other)], axis=1)
    down_sum = sum_team(wires, split(partial.astype(BF16)))
    result = middle + ordered(down_sum[:, :half], down_sum[:, half:])

    (hidden_moved,) = pick_columns(
        hidden_low, FF // shards, [[wires.place(me ^ m) for m in masks_of(back)]]
    )
    grad_low_own, grad_low_other = pick_columns(grad_low_team, half, [[core], [1 - core]])
    down_sent = wires.swap_core(through_low(hidden_moved, grad_low_other))
    down_keep = through_low(hidden_moved, grad_low_own).astype(F32) + down_sent.astype(F32)
    down_done = scatter_sum(wires, down_keep, back)

    gu_sent = wires.swap_core(through_low(second_moved, grad_other))
    gu_keep = through_low(second_moved, grad_own).astype(F32) + gu_sent.astype(F32)
    gu_done = scatter_sum(wires, gu_keep, back)
    gu_blocks = [gu_done[i * rows : (i + 1) * rows].astype(BF16) for i in range(4)]
    gu_back = [gu_blocks[0]] + [wires.swap(b, t) for b, t in zip(gu_blocks[1:], team[1:])]
    gu_sibling = wires.swap_core(jnp.concatenate(gu_back, axis=1))

    grad_middle_norm, post_gain_grad = norm_back(
        grad_second, second_normed, second_scale, post_gain
    )
    grad_middle = grad_out + grad_middle_norm
    grad_middle_low = both_packs(grad_middle.astype(BF16))
    grad_attn_moved = jnp.concatenate([against(grad_middle_low, w) for w in out_pieces], axis=1)
    position = {m: i for i, m in enumerate(out_rel)}
    table = jnp.asarray([position[m] for m in range(len(out_rel))], jnp.int32)
    group_blocks = GROUPS * HEAD_SIZE // rows
    grad_attn = pick_columns(
        grad_attn_moved.astype(BF16),
        rows,
        [
            [table[(me & below) ^ (g * group_blocks + j)] for j in range(group_blocks)]
            for g in range(per_core)
        ],
    )
    out_keep = scatter_sum(wires, through_low(attn_moved, grad_middle_low), out_back)
    out_got = wires.send(
        out_keep.astype(BF16), lambda s, c: (s ^ top, c) if (s & top != 0) != (c == 1) else None
    )
    out_low = out_keep + out_got.astype(F32)
    out_sibling = wires.send(
        out_low.astype(BF16), lambda s, c: (s, 1 - c) if (s & top != 0) == (c == 1) else None
    )
    out_done = jnp.where(at_home, out_low, out_sibling.astype(F32))

    grad_mixed, gain_grads = zip(
        *[attend_group_back(m, g, *packs, *gains) for m, g in zip(mixed, grad_attn)]
    )
    qkv_done = [
        scatter_sum(wires, through_low(x, g), order[::-1])
        for x, g, order in zip(first_moved, grad_mixed, orders)
    ]
    grad_first_part = spread_back(grad_mixed, qkv, block_places, rows)
    first_got = wires.swap_core(grad_first_part[PACK_CAPACITY:].astype(BF16))
    grad_first = grad_first_part[:PACK_CAPACITY] + first_got.astype(F32)
    grad_input_norm, in_gain_grad = norm_back(grad_first, first_normed, first_scale, in_gain)
    grad_tokens = (grad_middle + grad_input_norm).astype(BF16)

    gain_sum = sum(gain_grads)
    sums = jnp.concatenate(
        [in_gain_grad.reshape(-1, HEAD_SIZE), post_gain_grad.reshape(-1, HEAD_SIZE), gain_sum]
    )
    sums = sums + wires.swap_core(sums)
    for mask in wires.masks:
        sums = sums + wires.swap(sums, mask)
    lanes = d // HEAD_SIZE

    qkv_low = jnp.concatenate([v.astype(BF16) for v in qkv_done], axis=1)
    qkv_sibling = wires.swap_core(qkv_low)
    other_groups = [
        [GROUPS * (per_core * (1 - core) + g) + j for j in range(GROUPS)]
        + [
            QUERY_HEADS + per_core * (1 - core) + g,
            QUERY_HEADS + KEY_VALUE_HEADS + per_core * (1 - core) + g,
        ]
        for g in range(per_core)
    ]
    return (
        result.astype(BF16),
        grad_tokens,
        sums[:lanes].reshape(-1),
        sums[2 * lanes],
        sums[2 * lanes + 1],
        sums[lanes : 2 * lanes].reshape(-1),
        put_columns([qkv_low, qkv_sibling], HEAD_SIZE, [sum(column_groups, []), sum(other_groups, [])]),
        out_done,
        put_columns(
            gu_back + [gu_sibling],
            FF // shards,
            team_blocks(wires, core) + [sum(team_blocks(wires, 1 - core), [])],
        ),
        put_columns([down_done, wires.swap_core(down_done.astype(BF16))], half, [[core], [1 - core]]),
    )


def solution(mesh):
    shards, copies = mesh.shape["shard"], mesh.shape["replica"]
    body = lambda *args: on_device(shards, copies, *args)
    in_specs = (
        P(("shard", "replica"), None),
        P(("shard", "replica"), None),
        P(),
        P(),
        P(),
        P(),
        P("shard", None),
        P("shard", None),
        P("shard", None),
        P("shard", None),
        P(("shard", "replica"), None),
    )
    out_specs = (
        P(("shard", "replica"), None),
        P(("shard", "replica"), None),
        P(),
        P(),
        P(),
        P(),
        P("shard", None),
        P("shard", None),
        P("shard", None),
        P("shard", None),
    )
    return jax.shard_map(
        body, mesh=mesh, in_specs=in_specs, out_specs=out_specs, check_vma=False
    )
```

```python
import math

import jax
import jax.numpy as jnp
from jax import lax
from jax.experimental import pallas as pl
from jax.experimental.pallas import tpu as pltpu
from jax.sharding import PartitionSpec as P

QUERY_HEADS = 16
KEY_VALUE_HEADS = 8
HEAD_SIZE = 128
FF = 6144
PACK_CAPACITY = 256
NSEQ = 8
GROUPS = QUERY_HEADS // KEY_VALUE_HEADS


EPS = 1e-06
ROPE_BASE = 1000000.0
MASKED = -1e30
AXES = ("shard", "replica")
F32, BF16 = jnp.float32, jnp.bfloat16
SCALE = 1.0 / math.sqrt(HEAD_SIZE)
VMEM = 60 << 20
LIGHT = pl.CostEstimate(flops=1, bytes_accessed=1, transcendentals=0)


def pack_layout(lengths):
    ends = jnp.cumsum(lengths)
    starts = ends - lengths
    slots = jnp.arange(PACK_CAPACITY, dtype=jnp.int32)
    segment = jnp.sum((slots[:, None] >= ends[None, :]).astype(jnp.int32), axis=1)
    live = slots < ends[-1]
    labels = jnp.arange(NSEQ, dtype=jnp.int32)
    begin = jnp.sum(jnp.where(segment[:, None] == labels[None, :], starts[None, :], 0), axis=1)
    position = (slots - begin).astype(jnp.float32)
    segids = jnp.where(live, segment, NSEQ + slots)
    freqs = ROPE_BASE ** (-2.0 * jnp.arange(HEAD_SIZE // 2, dtype=jnp.float32) / HEAD_SIZE)
    angle = position[:, None] * freqs[None, :]
    cosine = jnp.concatenate([jnp.cos(angle), jnp.cos(angle)], axis=1)
    sine = jnp.concatenate([jnp.sin(angle), jnp.sin(angle)], axis=1)
    return (segids, cosine, sine, live)


def normalized_rows(value, gain):
    scale_inv = lax.rsqrt(jnp.mean(value * value, axis=-1, keepdims=True) + EPS)
    normed = value * scale_inv
    return (normed * gain, normed, scale_inv)


def norm_back(grad, normed, scale_inv, gain):
    scaled = grad * gain
    grad_in = scale_inv * (scaled - normed * jnp.mean(scaled * normed, axis=-1, keepdims=True))
    grad_gain = jnp.sum((grad * normed).reshape(-1, normed.shape[-1]), axis=0)
    return (grad_in, grad_gain)


def against(grad, matrix):
    return lax.dot_general(
        grad, matrix, (((1,), (1,)), ((), ())), preferred_element_type=jnp.float32
    )


def through(left, grad):
    return lax.dot_general(left, grad, (((0,), (0,)), ((), ())), preferred_element_type=jnp.float32)


class Wires:
    def __init__(self, shards, copies):
        self.shards, self.copies = shards, copies
        bits = shards.bit_length() - 1
        self.masks = [1 << b for b in range(bits)]
        self.top = shards >> 1
        self.team = [1, 4]
        self.far = [m for m in self.masks if m > 4]
        self.spread = [2] + self.far
        self.me = lax.axis_index("shard")
        self.core = lax.axis_index("replica")

    def send(self, value, to):
        pairs = []
        for i in range(self.shards * self.copies):
            goal = to(i // self.copies, i % self.copies)
            if goal is not None:
                pairs.append((i, goal[0] * self.copies + goal[1]))
        return lax.ppermute(value, AXES, pairs)

    def swap(self, value, mask):
        return self.send(value, lambda s, c: (s ^ mask, c))

    def swap_core(self, value):
        return self.send(value, lambda s, c: (s, 1 - c))

    def has(self, mask):
        return (self.me & mask) != 0

    def sharers(self):
        return self.groups(self.team)

    def teams(self):
        return self.groups(self.spread)

    def groups(self, fixed):
        fixed = sum(fixed)
        return [
            [s for s in range(self.shards) if s & fixed == f]
            for f in sorted({s & fixed for s in range(self.shards)})
        ]

    def others(self):
        return self.sharers()[0]


def masks_of(order):
    out = [0]
    for mask in reversed(order):
        out = out + [mask ^ m for m in out]
    return out


def pick_columns(value, block, groups):
    rows, width = value.shape
    places = jnp.stack([jnp.asarray(g, jnp.int32) for group in groups for g in group])
    if block % 128:
        blocks = value.reshape(rows, width // block, block)
        out, at = [], 0
        for group in groups:
            taken = jnp.take(blocks, places[at : at + len(group)], axis=1)
            out.append(taken.reshape(rows, len(group) * block))
            at += len(group)
        return out
    tile = math.gcd(rows, 256)

    def kernel(places_ref, in_ref, *out_refs):
        at = 0
        for group, out_ref in zip(groups, out_refs):
            for i in range(len(group)):
                start = pl.multiple_of(places_ref[at] * block, 128)
                out_ref[:, i * block : (i + 1) * block] = in_ref[:, pl.ds(start, block)]
                at += 1

    widths = [len(group) * block for group in groups]
    return list(
        pl.pallas_call(
            kernel,
            grid_spec=pltpu.PrefetchScalarGridSpec(
                num_scalar_prefetch=1,
                grid=(rows // tile,),
                in_specs=[pl.BlockSpec((tile, width), lambda i, s: (i, 0))],
                out_specs=[pl.BlockSpec((tile, w), lambda i, s: (i, 0)) for w in widths],
            ),
            out_shape=[jax.ShapeDtypeStruct((rows, w), value.dtype) for w in widths],
            compiler_params=pltpu.CompilerParams(vmem_limit_bytes=VMEM),
            cost_estimate=pl.CostEstimate(
                flops=0, bytes_accessed=2 * rows * (width + sum(widths)), transcendentals=0
            ),
            name="pick_columns",
        )(places, value)
    )


def put_columns(values, block, groups):
    rows = values[0].shape[0]
    places = jnp.stack([jnp.asarray(g, jnp.int32) for group in groups for g in group])
    width = block * places.shape[0]
    if block % 128:
        flat = jnp.concatenate([v.astype(F32) for v in values], axis=1)
        blocks = flat.reshape(rows, width // block, block)
        return jnp.zeros_like(blocks).at[:, places].set(blocks).reshape(rows, width)
    tile = math.gcd(rows, 64)

    def kernel(places_ref, *refs):
        out_ref, at = refs[-1], 0
        for group, ref in zip(groups, refs[:-1]):
            for i in range(len(group)):
                start = pl.multiple_of(places_ref[at] * block, 128)
                part = ref[:, i * block : (i + 1) * block]
                out_ref[:, pl.ds(start, block)] = part.astype(F32)
                at += 1

    return pl.pallas_call(
        kernel,
        grid_spec=pltpu.PrefetchScalarGridSpec(
            num_scalar_prefetch=1,
            grid=(rows // tile,),
            in_specs=[pl.BlockSpec((tile, v.shape[1]), lambda i, s: (i, 0)) for v in values],
            out_specs=pl.BlockSpec((tile, width), lambda i, s: (i, 0)),
        ),
        out_shape=jax.ShapeDtypeStruct((rows, width), F32),
        compiler_params=pltpu.CompilerParams(vmem_limit_bytes=VMEM),
        cost_estimate=LIGHT,
        name="put_columns",
    )(places, *values)


def after(value, *others):
    return lax.optimization_barrier((value, others))[0]


class Line:
    def __init__(self):
        self.last = ()

    def take(self, value):
        value = lax.optimization_barrier((value, self.last))[0]
        self.last = value
        return value

    def run(self, fn, *inputs):
        inputs = lax.optimization_barrier((inputs, self.last))[0]
        out = fn(*inputs)
        self.last = out
        return out

    def light(self, fn, *inputs, flags=()):
        return self.run(lambda *v: light(fn, *v, flags=flags), *inputs)


def ordered_pair(bit, own, other):
    return jnp.concatenate([jnp.where(bit, other, own), jnp.where(bit, own, other)], axis=0)


def scatter_sum(wires, keep, order):
    for mask in order:
        half = keep.shape[0] // 2
        got = wires.swap(keep[half:].astype(BF16), mask)
        keep = keep[:half].astype(F32) + got.astype(F32)
    return keep


def team_blocks(wires, half):
    one, two = wires.team
    mine = wires.me & (one | two)
    return [
        [half * wires.shards + ((mine ^ t) | s) for s in wires.others()]
        for t in (0, one, two, one | two)
    ]


def turned(value):
    return pltpu.roll(value, HEAD_SIZE // 2, 1)


def head_forward(raw, gain, cosine, sine):
    scale = lax.rsqrt(jnp.mean(raw * raw, axis=1, keepdims=True) + EPS)
    normed = raw * scale
    v = normed * gain
    return (v * cosine + turned(v) * sine).astype(BF16), normed, scale


def head_back(grad, normed, scale, gain, cosine, sine):
    g = grad * cosine + turned(grad * sine)
    scaled = g * gain
    raw = scale * (scaled - normed * jnp.mean(scaled * normed, axis=1, keepdims=True))
    return raw, jnp.sum(g * normed, axis=0, keepdims=True)


def attend_group(sources, cosine, sine, bias, q_gain, k_gain):
    tokens = sources[0][0].shape[0]
    packs = tokens // PACK_CAPACITY
    width = (GROUPS + 2) * HEAD_SIZE
    counts = [len(pieces) for _, pieces, _ in sources]
    columns = [c for _, _, c in sources]
    n_in = len(sources) + sum(counts)

    def kernel(*refs):
        cos_ref, sin_ref, bias_ref, qg_ref, kg_ref, attn_ref, mixed_ref = refs[n_in:]
        at, to = 0, 0
        for count, (start, stop) in zip(counts, columns):
            x_ref, w_refs = refs[at], refs[at + 1 : at + 1 + count]
            at += 1 + count
            depth = w_refs[0].shape[0]
            part = jnp.zeros((tokens, stop - start), F32)
            for i, w_ref in enumerate(w_refs):
                part += jnp.dot(
                    x_ref[:, i * depth : (i + 1) * depth], w_ref[:, start:stop],
                    preferred_element_type=F32,
                )
            mixed_ref[:, to : to + stop - start] = part
            to += stop - start
        for p in range(packs):
            at = slice(p * PACK_CAPACITY, (p + 1) * PACK_CAPACITY)
            cosine, sine, bias = cos_ref[at], sin_ref[at], bias_ref[at]
            head = lambda j: mixed_ref[at, j * HEAD_SIZE : (j + 1) * HEAD_SIZE]
            key, _, _ = head_forward(head(GROUPS), kg_ref[...], cosine, sine)
            value = head(GROUPS + 1).astype(BF16)
            for j in range(GROUPS):
                query, _, _ = head_forward(head(j), qg_ref[...], cosine, sine)
                scores = against(query, key) * SCALE + bias
                expd = jnp.exp(scores - jnp.max(scores, axis=1, keepdims=True))
                probs = expd / jnp.sum(expd, axis=1, keepdims=True)
                attn = jnp.dot(probs.astype(BF16), value, preferred_element_type=F32)
                attn_ref[at, j * HEAD_SIZE : (j + 1) * HEAD_SIZE] = attn.astype(BF16)

    d = sources[0][0].shape[1]
    return pl.pallas_call(
        kernel,
        out_shape=[
            jax.ShapeDtypeStruct((tokens, GROUPS * HEAD_SIZE), BF16),
            jax.ShapeDtypeStruct((tokens, width), F32),
        ],
        compiler_params=pltpu.CompilerParams(vmem_limit_bytes=VMEM),
        cost_estimate=LIGHT,
        name="attend_group",
    )(
        *[v for x, pieces, _ in sources for v in (x, *pieces)],
        cosine, sine, bias, q_gain, k_gain,
    )


def attend_group_back(mixed, grad, cosine, sine, bias, q_gain, k_gain):
    tokens, width = mixed.shape
    packs = tokens // PACK_CAPACITY

    def kernel(mixed_ref, grad_ref, cos_ref, sin_ref, bias_ref, qg_ref, kg_ref, out_ref, gain_ref):
        q_gain, k_gain = qg_ref[...], kg_ref[...]
        q_sum = jnp.zeros((1, HEAD_SIZE), F32)
        k_sum = jnp.zeros((1, HEAD_SIZE), F32)
        for p in range(packs):
            at = slice(p * PACK_CAPACITY, (p + 1) * PACK_CAPACITY)
            cosine, sine, bias = cos_ref[at], sin_ref[at], bias_ref[at]
            head = lambda j: mixed_ref[at, j * HEAD_SIZE : (j + 1) * HEAD_SIZE]
            key, key_normed, key_scale = head_forward(head(GROUPS), k_gain, cosine, sine)
            value = head(GROUPS + 1).astype(BF16)
            grad_key = jnp.zeros((PACK_CAPACITY, HEAD_SIZE), F32)
            grad_value = jnp.zeros((PACK_CAPACITY, HEAD_SIZE), F32)
            for j in range(GROUPS):
                cols = slice(j * HEAD_SIZE, (j + 1) * HEAD_SIZE)
                query, normed, scale = head_forward(head(j), q_gain, cosine, sine)
                g = grad_ref[at, cols]
                scores = against(query, key) * SCALE + bias
                expd = jnp.exp(scores - jnp.max(scores, axis=1, keepdims=True))
                probs = expd / jnp.sum(expd, axis=1, keepdims=True)
                dprobs = against(g, value)
                inner = jnp.sum(probs * dprobs, axis=1, keepdims=True)
                grad_scores = (probs * (dprobs - inner)).astype(BF16)
                grad_query = jnp.dot(grad_scores, key, preferred_element_type=F32) * SCALE
                grad_key += through(grad_scores, query)
                grad_value += through(probs.astype(BF16), g)
                raw, gain = head_back(grad_query, normed, scale, q_gain, cosine, sine)
                out_ref[at, cols] = raw.astype(BF16)
                q_sum += gain
            raw, gain = head_back(grad_key * SCALE, key_normed, key_scale, k_gain, cosine, sine)
            k_sum += gain
            out_ref[at, GROUPS * HEAD_SIZE : (GROUPS + 1) * HEAD_SIZE] = raw.astype(BF16)
            out_ref[at, (GROUPS + 1) * HEAD_SIZE :] = grad_value.astype(BF16)
        gain_ref[...] = jnp.concatenate([q_sum, k_sum] + [jnp.zeros_like(q_sum)] * 6, axis=0)

    return pl.pallas_call(
        kernel,
        out_shape=[
            jax.ShapeDtypeStruct((tokens, width), BF16),
            jax.ShapeDtypeStruct((8, HEAD_SIZE), F32),
        ],
        compiler_params=pltpu.CompilerParams(vmem_limit_bytes=VMEM),
        cost_estimate=LIGHT,
        name="attend_group_back",
    )(mixed, grad, cosine, sine, bias, q_gain, k_gain)


def spread_back(grads, weights, groups, block, dtype, parts, by_rows=False):
    tokens = grads[0].shape[0]
    width = sum(w.shape[0] for w in weights[0])
    places = jnp.stack([jnp.asarray(g, jnp.int32) for group in groups for g in group])
    if block % 128:
        total = 0.0
        for grad, pieces, group in zip(grads, weights, groups):
            part = jnp.concatenate([against(grad, w) for w in pieces], axis=1)
            total = total + put_columns([part], block, [group])
        return jnp.split(total.astype(dtype), parts, axis=0 if by_rows else 1)
    flat = [w for pieces in weights for w in pieces]
    shape = (tokens // parts, width) if by_rows else (tokens, width // parts)

    def kernel(places_ref, *refs):
        grad_refs, refs = refs[: len(grads)], refs[len(grads) :]
        out_ref, at, k = refs[-1], 0, 0
        out_refs = refs[-1 - parts : -1]
        for gi, grad_ref in enumerate(grad_refs):
            for _ in weights[gi]:
                part = against(grad_ref[...], refs[k][...])
                for b in range(part.shape[1] // block):
                    start = pl.multiple_of(places_ref[at] * block, 128)
                    cols = pl.ds(start, block)
                    new = part[:, b * block : (b + 1) * block]
                    out_ref[:, cols] = new if gi == 0 else out_ref[:, cols] + new
                    at += 1
                k += 1
        for i, ref in enumerate(out_refs):
            size = ref.shape[0] if by_rows else ref.shape[1]
            part = slice(i * size, (i + 1) * size)
            ref[...] = (out_ref[part, :] if by_rows else out_ref[:, part]).astype(dtype)

    whole = lambda v: pl.BlockSpec(v.shape, lambda i, s: (0, 0))
    return pl.pallas_call(
        kernel,
        grid_spec=pltpu.PrefetchScalarGridSpec(
            num_scalar_prefetch=1,
            grid=(1,),
            in_specs=[whole(v) for v in grads] + [whole(w) for w in flat],
            out_specs=[pl.BlockSpec(shape, lambda i, s: (0, 0))] * parts,
            scratch_shapes=[pltpu.VMEM((tokens, width), F32)],
        ),
        out_shape=[jax.ShapeDtypeStruct(shape, dtype)] * parts,
        compiler_params=pltpu.CompilerParams(vmem_limit_bytes=VMEM),
        cost_estimate=LIGHT,
        name="spread_back",
    )(places, *grads, *flat)


def feed_forward(second, own, other, grad_low, down_own, down_other, core):
    rows, d = second[0].shape
    n = len(second)
    tokens = n * rows
    units = down_own.shape[0]
    tile, half = 384, d // 2

    def kernel(core_ref, *refs):
        x_refs, go_refs, gx_refs = refs[:n], refs[n : 2 * n], refs[2 * n : 3 * n]
        own_ref, other_ref, do_ref, dx_ref, hidden_ref, out_own_ref, out_other_ref = refs[3 * n :]
        first = core_ref[0] == 0
        for r in range(n):
            at = slice(r * rows, (r + 1) * rows)
            x = x_refs[r][...]
            a = jnp.dot(x, own_ref[...], preferred_element_type=F32)
            b = jnp.dot(x, other_ref[...], preferred_element_type=F32)
            gate, upward = jnp.where(first, a, b), jnp.where(first, b, a)
            sigma = jax.nn.sigmoid(gate)
            silu = gate * sigma
            hidden_ref[at, :] = (silu * upward).astype(BF16)
            grad = against(go_refs[r][...], do_ref[...]) + against(gx_refs[r][...], dx_ref[...])
            grad_gate = grad * upward * sigma * (1.0 + gate * (1.0 - sigma))
            grad_up = grad * silu
            out_own_ref[at, :] = jnp.where(first, grad_gate, grad_up).astype(BF16)
            out_other_ref[at, :] = jnp.where(first, grad_up, grad_gate).astype(BF16)

    once = pl.Buffered(1)
    in_specs = [pl.BlockSpec((rows, d), lambda j, s: (0, 0), pipeline_mode=once)] * n
    in_specs += [pl.BlockSpec((rows, half), lambda j, s: (0, s[0]), pipeline_mode=once)] * n
    in_specs += [pl.BlockSpec((rows, half), lambda j, s: (0, 1 - s[0]), pipeline_mode=once)] * n
    in_specs += [pl.BlockSpec((d, tile), lambda j, s: (0, j))] * 2
    in_specs += [pl.BlockSpec((tile, half), lambda j, s: (j, 0))] * 2
    return pl.pallas_call(
        kernel,
        grid_spec=pltpu.PrefetchScalarGridSpec(
            num_scalar_prefetch=1,
            grid=(units // tile,),
            in_specs=in_specs,
            out_specs=[pl.BlockSpec((tokens, tile), lambda j, s: (0, j))] * 3,
        ),
        out_shape=[jax.ShapeDtypeStruct((tokens, units), BF16)] * 3,
        compiler_params=pltpu.CompilerParams(vmem_limit_bytes=VMEM),
        cost_estimate=LIGHT,
        name="feed_forward",
    )(core.reshape(1), *second, *grad_low, *grad_low, own, other, down_own, down_other)


def feed_forward_back(grad_own, grad_other, own, other, places, block, n):
    tokens, units = grad_own.shape
    d = own.shape[0]
    rows = tokens // n
    if block % 128:
        part = against(grad_own, own) + against(grad_other, other)
        part = put_columns([part], block, [places]).astype(BF16)
        return [part[i * rows : (i + 1) * rows] for i in range(n)]
    width = 512

    def kernel(go_ref, gx_ref, own_ref, other_ref, *out_refs):
        for at in range(0, d, width):
            part = against(go_ref[...], own_ref[at : at + width, :])
            part += against(gx_ref[...], other_ref[at : at + width, :])
            part = part.astype(BF16)
            for b in range(width // block):
                to = places[at // block + b] * block
                for i in range(n):

                    @pl.when(pl.program_id(0) == (n - 1 - i) // 2)
                    def _(i=i, b=b, to=to):
                        row = (i % 2) * rows
                        out_refs[i][:, to : to + block] = part[
                            row : row + rows, b * block : (b + 1) * block
                        ]

    return pl.pallas_call(
        kernel,
        grid=(n // 2,),
        in_specs=[pl.BlockSpec((2 * rows, units), lambda i: (n // 2 - 1 - i, 0))] * 2
        + [pl.BlockSpec(own.shape, lambda i: (0, 0), pipeline_mode=pl.Buffered(1))] * 2,
        out_specs=[pl.BlockSpec((rows, d), lambda i: (0, 0))] * n,
        out_shape=[jax.ShapeDtypeStruct((rows, d), BF16)] * n,
        compiler_params=pltpu.CompilerParams(vmem_limit_bytes=VMEM),
        cost_estimate=LIGHT,
        name="feed_forward_back",
    )(grad_own, grad_other, own, other)


def weight_grad(lefts, tile, rights, column, width, added=None, split=False):
    units = lefts[0].shape[1]
    n, m = len(lefts), len(rights)
    steps = units // tile
    row_of = lambda vs, at: next(
        (i, at - sum(v.shape[0] for v in vs[:i]))
        for i in range(len(vs))
        if at < sum(v.shape[0] for v in vs[: i + 1])
    )
    tokens = sum(v.shape[0] for v in lefts)
    piece = min(v.shape[0] for v in [*lefts, *rights])

    def kernel(column_ref, *refs):
        left_refs, right_refs = refs[:n], refs[n : n + m]
        total = None
        for at in range(0, tokens, piece):
            (i, a), (j, b) = row_of(lefts, at), row_of(rights, at)
            part = through(left_refs[i][a : a + piece, :], right_refs[j][b : b + piece, :])
            total = part if total is None else total + part
        if added is not None:
            total += refs[n + m][...].astype(F32)
        if not split:
            refs[-1][...] = total.astype(BF16)
        else:

            @pl.when(pl.program_id(0) < steps // 2)
            def _():
                refs[-2][...] = total.astype(BF16)

            @pl.when(pl.program_id(0) >= steps // 2)
            def _():
                refs[-1][...] = total.astype(BF16)

    extra = [] if added is None else [added]
    once = pl.Buffered(1)
    half = steps // 2
    if split:
        out_specs = [
            pl.BlockSpec((tile, width), lambda i, s: (jnp.minimum(i, half - 1), 0)),
            pl.BlockSpec((tile, width), lambda i, s: (jnp.maximum(i - half, 0), 0)),
        ]
        out_shape = [jax.ShapeDtypeStruct((units // 2, width), BF16)] * 2
    else:
        out_specs = pl.BlockSpec((tile, width), lambda i, s: (i, 0))
        out_shape = jax.ShapeDtypeStruct((units, width), BF16)
    return pl.pallas_call(
        kernel,
        grid_spec=pltpu.PrefetchScalarGridSpec(
            num_scalar_prefetch=1,
            grid=(steps,),
            in_specs=[pl.BlockSpec((v.shape[0], tile), lambda i, s: (0, i)) for v in lefts]
            + [
                pl.BlockSpec((v.shape[0], width), lambda i, s: (0, s[0]), pipeline_mode=once)
                for v in rights
            ]
            + [pl.BlockSpec((tile, width), lambda i, s: (i, 0))] * len(extra),
            out_specs=out_specs,
        ),
        out_shape=out_shape,
        compiler_params=pltpu.CompilerParams(vmem_limit_bytes=VMEM),
        cost_estimate=LIGHT,
        name="weight_grad",
    )(jnp.asarray(column, jnp.int32).reshape(1), *lefts, *rights, *extra)


def down_project(hidden, own, other):
    tokens, units = hidden.shape
    half = own.shape[1]
    n = 4
    rows = tokens // n

    def kernel(hidden_ref, own_ref, other_ref, *out_refs):
        for r, out_ref in enumerate(out_refs):

            @pl.when(pl.program_id(0) == r)
            def _(out_ref=out_ref):
                for i, ref in enumerate((own_ref, other_ref)):
                    part = jnp.dot(hidden_ref[...], ref[...], preferred_element_type=F32)
                    out_ref[:, i * half : (i + 1) * half] = part.astype(BF16)

    once = pl.Buffered(1)
    return pl.pallas_call(
        kernel,
        grid=(n,),
        in_specs=[pl.BlockSpec((rows, units), lambda i: (i, 0))]
        + [pl.BlockSpec((units, half), lambda i: (0, 0), pipeline_mode=once)] * 2,
        out_specs=[pl.BlockSpec((rows, 2 * half), lambda i: (0, 0))] * n,
        out_shape=[jax.ShapeDtypeStruct((rows, 2 * half), BF16)] * n,
        compiler_params=pltpu.CompilerParams(vmem_limit_bytes=VMEM),
        cost_estimate=LIGHT,
        name="down_project",
    )(hidden, own, other)


def light(fn, *args, flags=()):
    flat, tree = jax.tree.flatten(args)
    n = len(flags)
    shapes = jax.eval_shape(lambda *v: fn(*[jnp.bool_(True)] * n, *v), *args)
    out_flat, out_tree = jax.tree.flatten(shapes)

    def kernel(*refs):
        flag_ref, refs = refs[0], refs[1:]
        values = jax.tree.unflatten(tree, [r[...] for r in refs[: len(flat)]])
        out = fn(*[flag_ref[i] != 0 for i in range(n)], *values)
        for ref, value in zip(refs[len(flat) :], jax.tree.leaves(out)):
            ref[...] = value

    bits = jnp.stack([jnp.asarray(f, jnp.int32) for f in (*flags, True)])
    whole = lambda v: pl.BlockSpec(v.shape, lambda i, s, r=len(v.shape): (0,) * r)
    out = pl.pallas_call(
        kernel,
        grid_spec=pltpu.PrefetchScalarGridSpec(
            num_scalar_prefetch=1,
            grid=(1,),
            in_specs=[whole(v) for v in flat],
            out_specs=[whole(v) for v in out_flat],
        ),
        out_shape=[jax.ShapeDtypeStruct(v.shape, v.dtype) for v in out_flat],
        compiler_params=pltpu.CompilerParams(vmem_limit_bytes=VMEM),
        cost_estimate=LIGHT,
        name="light",
    )(bits, *flat)
    return jax.tree.unflatten(out_tree, out)


def tables(lengths):
    segids, cosine, sine, live = pack_layout(lengths)
    slots = jnp.arange(PACK_CAPACITY, dtype=jnp.int32)
    allowed = (segids[:, None] == segids[None, :]) & (slots[:, None] >= slots[None, :])
    half = HEAD_SIZE // 2
    sine = jnp.concatenate([-sine[:, :half], sine[:, half:]], axis=1)
    return cosine, sine, jnp.where(allowed, 0.0, MASKED).astype(F32), live


def on_device(
    shards,
    copies,
    tokens,
    seq_lengths,
    in_gain,
    q_gain,
    key_norm_gain,
    post_gain,
    w_qkv,
    w_out,
    w_gate_up,
    w_down,
    cotangent,
):
    wires = Wires(shards, copies)
    me, core, top = wires.me, wires.core, wires.top
    first_core = core == 0
    rows = w_qkv.shape[0]
    d = in_gain.shape[0]
    half = d // 2
    by_core = lambda own, other: (jnp.where(first_core, own, other), jnp.where(first_core, other, own))
    ordered = lambda own, other: jnp.concatenate(by_core(own, other), axis=-1)
    dot = lambda a, b: jnp.dot(a, b, preferred_element_type=F32)
    through_low = lambda a, b: through(a, b).astype(BF16)
    both_packs = lambda v: jnp.concatenate([v, wires.swap_core(v)], axis=0)

    per_core = KEY_VALUE_HEADS // 2
    one, two = wires.team
    x, y, z = 1, 2, 4
    line = Line()
    stack = lambda *parts: jnp.concatenate(parts, axis=0)
    swap, swap_core = wires.swap, wires.swap_core
    low = lambda v: v.astype(BF16)
    wide = lambda v: v.astype(F32)

    def halves(v):
        n = v.shape[0] // 2
        return v[:n], v[n:]

    def head_blocks(core):
        return [
            [GROUPS * (per_core * core + g) + j for j in range(GROUPS)]
            + [QUERY_HEADS + per_core * core + g, QUERY_HEADS + KEY_VALUE_HEADS + per_core * core + g]
            for g in range(per_core)
        ]

    def parcels(core):
        by = head_blocks(core)
        return [by[0] + by[3][:GROUPS], by[1] + by[3][GROUPS:], by[2]]

    qkv_orders = [wires.far + o for o in ([z, x, y], [y, z, x], [x, y, z])]
    widths = [len(p) * HEAD_SIZE for p in parcels(core)]
    starts = [sum(widths[:i]) for i in range(len(widths))]

    lengths_got = swap_core(seq_lengths.astype(F32))
    gu_parts = line.run(
        lambda w: pick_columns(w, FF // shards, team_blocks(wires, core)), w_gate_up
    )
    gu_got = [swap(p, t) for p, t in zip(gu_parts[1:], (one, two, one | two))]
    (qkv_rows,) = line.run(
        lambda w: pick_columns(w, HEAD_SIZE, [sum(parcels(core), [])]), w_qkv
    )
    qkv_got = swap(qkv_rows, wires.far[0])
    lengths_got = line.take(lengths_got)
    row = lambda v: v.reshape(1, -1)
    first_own = line.light(
        lambda v, g: low(normalized_rows(wide(v), g)[0]), tokens, row(in_gain)
    )
    first_other = swap_core(first_own)
    at_home = wires.has(top) == (core == 1)
    away_to = lambda s, c: (s ^ top, c) if (s & top != 0) == (c == 1) else None
    cosine, sine, bias, live = tables(seq_lengths[0])
    lengths_other = lengths_got[0].astype(jnp.int32)
    packs = [
        jnp.concatenate(pair, axis=0)
        for pair in zip((cosine, sine, bias), tables(lengths_other)[:3])
    ]
    gains = [q_gain.reshape(1, -1), key_norm_gain.reshape(1, -1)]
    live = live[:, None].astype(F32)
    packs, live = line.run(lambda *v: v, packs, live)
    grad_low = line.light(lambda v, k: low(wide(v) * k), cotangent, live)
    (down_half,) = line.run(lambda w: pick_columns(w, half, [[core]]), w_down)
    gu_got, qkv_got, first_other = line.take((gu_got, qkv_got, first_other))

    def team_rows(has_one, has_two, own, by_one, by_two, by_both):
        near = ordered_pair(has_one, own, by_one)
        return ordered_pair(has_two, near, ordered_pair(has_one, by_two, by_both))

    team_flags = (wires.has(one), wires.has(two))
    for mask in wires.far:
        got = qkv_got if mask == wires.far[0] else line.take(swap(qkv_rows, mask))
        qkv_rows = line.light(stack, qkv_rows, got)
    legs = line.light(lambda v: [v[:, at : at + w] for at, w in zip(starts, widths)], qkv_rows)
    leg = len(wires.far)
    got = [swap(v, o[leg]) for v, o in zip(legs, qkv_orders)]
    away = wires.send(w_out, away_to)
    down_y = swap(line.take(down_half), y)
    gu_rows = line.light(
        lambda *v: halves(team_rows(*v)), gu_parts[0], *gu_got, flags=team_flags
    )
    gu_a, gu_b = gu_rows

    def spread_far(v):
        out = [v]
        for mask in wires.far:
            out = out + [swap(p, mask) for p in out]
        return out

    block_places = [[me ^ m for m in masks_of(order[::-1])] for order in qkv_orders]
    first_low = line.light(stack, first_own, first_other)
    first_moved = line.run(lambda v: pick_columns(v, rows, block_places), first_low)
    join = lambda a, b: [stack(v, g) for v, g in zip(a, b)]
    legs = line.light(join, legs, line.take(got))
    got = [swap(v, o[leg + 1]) for v, o in zip(legs, qkv_orders)]
    gu_a = spread_far(gu_a)
    got, away, down_y = line.take((got, away, down_y))
    legs = line.light(join, legs, got)
    got = [swap(v, o[leg + 2]) for v, o in zip(legs, qkv_orders)]
    out_legs = line.light(
        lambda home, v, w: jnp.where(home, w, v), away, w_out, flags=(at_home,)
    )
    got, gu_a = line.take((got, gu_a))
    qkv = [[v, g] for v, g in zip(legs, got)]

    out_masks = [m for m in wires.far if m != top]
    out_orders = [out_masks + o for o in ([z, x, y], [z, y, x])]
    for mask in out_masks:
        out_legs = line.light(stack, out_legs, line.take(swap(out_legs, mask)))
    out_legs, grad_low = line.take((out_legs, grad_low))
    got = swap(out_legs, z)
    grad_low_one = swap(grad_low, one)
    grad_low_two = swap(grad_low, two)
    gu_a_y = [swap(gu_a[0], y)]
    gu_b = spread_far(line.take(gu_b))
    attn, mixed = [], []

    def attend(g):
        if g < 3:
            sources = [(first_moved[g], qkv[g], (0, (GROUPS + 2) * HEAD_SIZE))]
        else:
            at = (GROUPS + 2) * HEAD_SIZE
            sources = [
                (first_moved[i], qkv[i], (at, at + GROUPS * HEAD_SIZE)) for i in range(2)
            ]
        out = line.run(
            lambda cosine: attend_group(sources, cosine, *packs[1:], *gains), packs[0]
        )
        attn.append(out[0])
        mixed.append(out[1])

    attend(0)
    attend(1)
    got, grad_low_one, gu_a_y[0] = line.take((got, grad_low_one, gu_a_y[0]))
    out_legs = line.light(
        lambda v, g: [stack(v, g)[:, i * half : (i + 1) * half] for i in range(2)], out_legs, got
    )
    got = [swap(v, o[-2]) for v, o in zip(out_legs, out_orders)]
    gu_b_y = [swap(line.take(gu_b[0]), y)]
    attend(2)
    attend(3)
    gu_b = line.take(gu_b)
    down_far = spread_far(line.take(down_half))
    got, grad_low_two, gu_b_y[0] = line.take((got, grad_low_two, gu_b_y[0]))
    out_legs = line.light(join, out_legs, got)
    got = [swap(v, o[-1]) for v, o in zip(out_legs, out_orders)]
    gu_a_y = gu_a_y + [swap(v, y) for v in line.take(gu_a[1:])]
    grad_low_both = swap(line.take(grad_low_one), two)
    below = top - 1
    out_places = [[(me & below) ^ m for m in masks_of(o[::-1])] for o in out_orders]
    attn = line.light(lambda *v: jnp.concatenate(v, axis=1), *attn)
    attn_moved = line.run(lambda v: pick_columns(v, rows, out_places), attn)
    got, grad_low_both, down_far = line.take((got, grad_low_both, down_far))
    out_w = [[v, g] for v, g in zip(out_legs, got)]

    def project_out(moved, weights):
        parts = []
        for v, w in zip(moved, weights):
            depth = w[0].shape[0]
            parts.append(sum(dot(v[:, i * depth : (i + 1) * depth], p) for i, p in enumerate(w)))
        part = jnp.concatenate(parts, axis=1)
        return part[:PACK_CAPACITY], low(part[PACK_CAPACITY:])

    out_part, out_send = line.light(project_out, attn_moved, out_w)
    out_got = line.take(swap_core(out_send))
    columns = [f | t for f in wires.sharers()[0] for t in (0, one, two, one | two)]

    def to_second(v, part, got, gain):
        middle = wide(v) + (part + wide(got))
        second = low(normalized_rows(middle, gain)[0])
        return middle, jnp.concatenate([second[:, c * rows : (c + 1) * rows] for c in columns], axis=1)

    middle, second_low = line.light(to_second, tokens, out_part, out_got, row(post_gain))

    second_two = swap(second_low, two)
    second_one = swap(second_low, one)
    gu_b_y = gu_b_y + [swap(v, y) for v in gu_b[1:]]
    down_far_y = [down_y] + [swap(v, y) for v in down_far[1:]]
    gu_a_y, gu_b_y, second_two = line.take((gu_a_y, gu_b_y, second_two))
    second_both = swap(second_two, one)
    second_one, second_both, down_far_y = line.take((second_one, second_both, down_far_y))
    order_flags = [wires.has(y)] + [wires.has(mask) for mask in wires.far]

    def in_order(*v):
        flags, (near, by_y) = v[: len(order_flags)], v[len(order_flags) :]
        rows_of = [ordered_pair(flags[0], a, b) for a, b in zip(near, by_y)]
        for flag in flags[1:]:
            rows_of = [ordered_pair(flag, a, b) for a, b in zip(rows_of[::2], rows_of[1::2])]
        return rows_of[0]

    gu_own = line.light(
        lambda *v: in_order(
            *v[: len(order_flags)],
            *[
                [jnp.concatenate(pair, axis=0) for pair in zip(a, b)]
                for a, b in (v[-4:-2], v[-2:])
            ],
        ),
        gu_a, gu_b, gu_a_y, gu_b_y, flags=order_flags,
    )
    gu_other = swap_core(gu_own)
    down_own = line.light(in_order, down_far, down_far_y, flags=order_flags)
    down_other = swap_core(down_own)
    gu_other, down_other = line.take((gu_other, down_other))

    second_team = [second_low, second_two, second_one, second_both]
    grad_low_team = [grad_low, grad_low_two, grad_low_one, grad_low_both]
    hidden_low, grad_own, grad_other = line.run(
        lambda v, g: feed_forward(v, gu_own, gu_other, g, down_own, down_other, core),
        second_team, grad_low_team,
    )
    def down_blocks(has_y, v):
        n = v.shape[0] // (shards // 4)
        by = [v[i * n : (i + 1) * n] for i in range(shards // 4)]
        low_y, high_y = jnp.concatenate(by[::2], axis=0), jnp.concatenate(by[1::2], axis=0)
        return jnp.where(has_y, high_y, low_y), jnp.where(has_y, low_y, high_y)

    def far_blocks(has_far, mine, got):
        one_half, other_half = halves(wide(mine) + wide(got))
        return (
            jnp.where(has_far, other_half, one_half),
            low(jnp.where(has_far, one_half, other_half)),
        )

    units = hidden_low.shape[1]
    gu_sent = swap_core(
        line.run(lambda g: weight_grad(second_team, 512, [g], 0, units), grad_other)
    )
    down_sent = swap_core(
        line.run(lambda h: weight_grad([h], 384, grad_low_team, 1 - core, half), hidden_low)
    )
    share_own, share_two, share_one, share_both = line.run(
        lambda a, b: feed_forward_back(a, b, gu_own, gu_other, columns, rows, 4),
        grad_own, grad_other,
    )
    got_two = swap(share_both, one)

    gu_sent, down_sent = line.take((gu_sent, down_sent))
    gu_keep = line.run(
        lambda g, sent: weight_grad(second_team, 512, [g], 0, units, sent), grad_own, gu_sent
    )
    gu_keep = line.light(
        lambda has_y, v: down_blocks(has_y, v), gu_keep, flags=(wires.has(y),)
    )
    gu_got = swap(gu_keep[1], y)
    got_two = line.take(got_two)
    got_last = swap(line.light(lambda a, b: low(wide(a) + wide(b)), share_two, got_two), two)
    got_own = swap(line.take(share_one), one)
    down_keep = line.run(
        lambda h, sent: weight_grad([h], 384, grad_low_team, core, half, sent), hidden_low, down_sent
    )
    down_keep = line.light(
        lambda has_y, v: down_blocks(has_y, v), down_keep, flags=(wires.has(y),)
    )
    down_got = swap(down_keep[1], y)
    part_own, part_two, part_one, part_both = line.run(
        lambda h: down_project(h, down_own, down_other), hidden_low
    )
    got_own, got_last = line.take((got_own, got_last))

    def norm_gradient(parts, v, gain):
        _, normed, scale = normalized_rows(v, gain)
        grad = sum(wide(p) for p in parts)
        scaled = grad * gain
        mean = jnp.mean(scaled * normed, axis=-1, keepdims=True)
        return scale * (scaled - normed * mean), jnp.sum(grad * normed, axis=0, keepdims=True)

    def to_middle(parts, v, gain, cotangent, live):
        norm_part, gain_part = norm_gradient(parts, v, gain)
        grad = wide(cotangent) * live + norm_part
        return grad, low(grad), gain_part

    grad_middle, grad_middle_own, post_gain_grad = line.light(
        to_middle, (share_own, got_own, got_last), middle, row(post_gain), cotangent, live
    )
    grad_middle_other = swap_core(grad_middle_own)
    part_got_two = swap(line.take(part_both), one)
    grad_middle_low, *out_cols = line.light(
        lambda a, b: (stack(a, b), stack(a, b)[:, :half], stack(a, b)[:, half:]),
        grad_middle_own, line.take(grad_middle_other),
    )
    grad_attn = line.run(
        lambda *cols: spread_back(cols, out_w, out_places, rows, BF16, per_core), *out_cols
    )
    n_out = attn_moved[0].shape[1]
    out_back = [x, z, y] + out_masks[::-1]
    attn_back = line.run(
        lambda v: pick_columns(v, rows, [[(me & below) ^ m for m in masks_of(out_back)]])[0], attn
    )
    grad_mixed, gain_grads = {}, []

    def attend_back(g):
        got = line.run(
            lambda v: attend_group_back(
                mixed[g],
                v[g],
                *packs,
                *gains,
            ),
            grad_attn,
        )
        grad_mixed[g] = got[0]
        gain_grads.append(got[1])

    q_width = GROUPS * HEAD_SIZE
    qkv_back = [o[::-1] for o in qkv_orders]

    def next_step(keep, got):
        mine, away = halves(wide(keep) + wide(got))
        return mine, low(away)

    def far_step(keep, got):
        for mask in wires.far[::-1]:
            keep, away = line.light(far_blocks, keep, got, flags=(wires.has(mask),))
            got = swap(away, mask)
            if mask != wires.far[0]:
                got = line.take(got)
        return keep, got

    def parcel_back(g, *extra):
        parcel = grad_mixed[g]
        if extra:
            parcel = line.light(lambda *v: jnp.concatenate(v, axis=1), parcel, *extra)
        keep = line.run(
            lambda v, p: weight_grad([v], 512, [p], 0, p.shape[1], split=True),
            first_moved[g], parcel,
        )
        return parcel, keep, swap(keep[1], qkv_back[g][0])

    def add_step(keep, got, mask):
        keep = line.light(next_step, keep[0], line.take(got))
        return keep, swap(keep[1], mask)

    attend_back(3)
    last_q, last_kv = line.light(lambda v: (v[:, :q_width], v[:, q_width:]), grad_mixed[3])
    attend_back(1)
    part_got_two = line.take(part_got_two)
    part_got_last = swap(line.light(lambda a, b: low(wide(a) + wide(b)), part_two, part_got_two), two)
    part_got_own = swap(line.take(part_one), one)
    parcels_back = {1: parcel_back(1, last_kv)}
    attend_back(2)
    parcels_back[2] = parcel_back(2)
    out_keep = line.run(
        lambda v: weight_grad([v], n_out // 4, [grad_middle_low], 0, d, split=True), attn_back
    )
    out_got = swap(out_keep[1], out_back[0])
    attend_back(0)
    part_got_own, part_got_last = line.take((part_got_own, part_got_last))

    def to_result(own_first, m, parts):
        total = sum(wide(v) for v in parts)
        a, b = total[:, :half], total[:, half:]
        columns = [jnp.where(own_first, a, b), jnp.where(own_first, b, a)]
        return low(m + jnp.concatenate(columns, axis=1))

    result = line.light(
        to_result, middle, (part_own, part_got_own, part_got_last), flags=(first_core,)
    )
    gu_got, down_got = line.take((gu_got, down_got))
    gu_mine, gu_far_got = far_step(gu_keep[0], gu_got)
    parcels_back[0] = parcel_back(0, last_q)
    grad_parcels = [parcels_back[g][0] for g in range(3)]
    keeps = [parcels_back[g][1] for g in range(3)]
    gots = [parcels_back[g][2] for g in range(3)]
    keeps[1], gots[1] = add_step(keeps[1], gots[1], qkv_back[1][1])
    keeps[2], gots[2] = add_step(keeps[2], gots[2], qkv_back[2][1])
    grad_first_part = line.run(
        lambda *g: spread_back(g, qkv, block_places, rows, BF16, 2, True), *grad_parcels
    )
    keeps[0], gots[0] = add_step(keeps[0], gots[0], qkv_back[0][1])
    keeps[1], gots[1] = add_step(keeps[1], gots[1], qkv_back[1][2])
    keeps[2], gots[2] = add_step(keeps[2], gots[2], qkv_back[2][2])
    out_keep, out_got = add_step(out_keep, out_got, out_back[1])
    gu_far_got = line.take(gu_far_got)
    gu_half = line.light(lambda a, b: low(a + wide(b)), gu_mine, gu_far_got)
    down_mine, down_got = far_step(down_keep[0], down_got)
    first_got = line.take(swap_core(grad_first_part[1]))

    def to_tokens(parts, v, gain, grad):
        norm_part, gain_part = norm_gradient(parts, wide(v), gain)
        return low(grad + norm_part), gain_part

    grad_tokens, in_gain_grad = line.light(
        to_tokens, (grad_first_part[0], first_got), tokens, row(in_gain), grad_middle
    )
    sums = jnp.concatenate(
        [
            in_gain_grad.reshape(-1, HEAD_SIZE),
            post_gain_grad.reshape(-1, HEAD_SIZE),
            sum(gain_grads),
        ]
    )
    keeps[0], gots[0] = add_step(keeps[0], gots[0], qkv_back[0][2])
    sums = sums + line.take(swap_core(sums))
    out_keep, out_got = add_step(out_keep, out_got, out_back[2])
    keeps = line.light(
        lambda a, b: [wide(k[0]) + wide(g) for k, g in zip(a, b)], keeps, line.take(gots)
    )
    cut = lambda v: (halves(v)[0], low(halves(v)[1]))
    mine, away = line.light(lambda *v: cut(jnp.concatenate(v, axis=1)), *keeps)
    for mask in wires.far[::-1]:
        last_got = swap(away, mask)
        if mask != wires.far[0]:
            mine, away = line.light(lambda a, b: cut(a + wide(b)), mine, line.take(last_got))
    def return_rows(has_one, has_two, v):
        by = [v[i * rows : (i + 1) * rows] for i in range(4)]
        near = [jnp.where(has_two, by[i + 2], by[i]) for i in range(2)]
        away = [jnp.where(has_two, by[i], by[i + 2]) for i in range(2)]
        pick = lambda pair: [
            jnp.where(has_one, pair[1], pair[0]), jnp.where(has_one, pair[0], pair[1])
        ]
        return pick(near) + pick(away)

    gu_back = line.light(return_rows, gu_half, flags=team_flags)
    gu_back[1:] = [swap(b, t) for b, t in zip(gu_back[1:], (one, two, one | two))]
    sums_got = swap(line.take(sums), wires.masks[0])
    down_got = line.take(down_got)
    down_done = line.light(lambda a, b: low(a + wide(b)), down_mine, down_got)
    down_sibling = swap_core(down_done)
    gu_back[1:] = line.take(gu_back[1:])
    gu_sibling = swap_core(line.light(lambda *v: jnp.concatenate(v, axis=1), *gu_back))
    out_got = line.take(out_got)
    out_done = line.light(lambda a, b: wide(a) + wide(b), out_keep[0], out_got)
    out_done = scatter_sum(wires, out_done, out_back[3:])
    out_away = line.light(low, out_done)
    back_to = lambda s, c: (s ^ top, c) if (s & top != 0) != (c == 1) else None
    out_got = wires.send(out_away, back_to)
    sums = sums + line.take(sums_got)
    sums_got = swap(sums, wires.masks[1])
    last_got, down_sibling, gu_sibling = line.take((last_got, down_sibling, gu_sibling))
    qkv_done = line.light(lambda a, b: low(a + wide(b)), mine, last_got)
    qkv_sibling = swap_core(qkv_done)
    sums = sums + line.take(sums_got)
    sums_got = swap(sums, wires.masks[2])
    gu_out = line.run(
        lambda *v: put_columns(
            list(v),
            FF // shards,
            team_blocks(wires, core) + [sum(team_blocks(wires, 1 - core), [])],
        ),
        *gu_back, gu_sibling,
    )
    out_low = line.light(lambda a, b: low(a + wide(b)), out_done, line.take(out_got))
    out_sibling = wires.send(
        out_low, lambda s, c: (s, 1 - c) if (s & top != 0) == (c == 1) else None
    )
    sums = sums + line.take(sums_got)
    sums_got = swap(sums, wires.masks[3])
    down_out = line.run(
        lambda a, b: put_columns([a, b], half, [[core], [1 - core]]), down_done, down_sibling
    )
    qkv_out = line.run(
        lambda a, b: put_columns(
            [a, b], HEAD_SIZE, [sum(parcels(core), []), sum(parcels(1 - core), [])]
        ),
        qkv_done, line.take(qkv_sibling),
    )
    out_done = line.light(
        lambda home, a, b: wide(jnp.where(home, a, b)),
        out_low, line.take(out_sibling), flags=(at_home,),
    )
    sums = sums + line.take(sums_got)
    for mask in wires.masks[4:]:
        sums = sums + line.take(swap(sums, mask))
    lanes = d // HEAD_SIZE

    return (
        result,
        grad_tokens,
        sums[:lanes].reshape(-1),
        sums[2 * lanes],
        sums[2 * lanes + 1],
        sums[lanes : 2 * lanes].reshape(-1),
        qkv_out,
        out_done,
        gu_out,
        down_out,
    )


def solution(mesh):
    shards, copies = mesh.shape["shard"], mesh.shape["replica"]
    body = lambda *args: on_device(shards, copies, *args)
    in_specs = (
        P(("shard", "replica"), None),
        P(("shard", "replica"), None),
        P(),
        P(),
        P(),
        P(),
        P("shard", None),
        P("shard", None),
        P("shard", None),
        P("shard", None),
        P(("shard", "replica"), None),
    )
    out_specs = (
        P(("shard", "replica"), None),
        P(("shard", "replica"), None),
        P(),
        P(),
        P(),
        P(),
        P("shard", None),
        P("shard", None),
        P("shard", None),
        P("shard", None),
    )
    return jax.shard_map(
        body, mesh=mesh, in_specs=in_specs, out_specs=out_specs, check_vma=False
    )
```

```python
import math

import jax
import jax.numpy as jnp
from jax import lax
from jax.experimental import pallas as pl
from jax.experimental.pallas import tpu as pltpu
from jax.sharding import PartitionSpec as P

QUERY_HEADS = 16
KEY_VALUE_HEADS = 8
HEAD_SIZE = 128
FF = 6144
PACK_CAPACITY = 256
NSEQ = 8
GROUPS = QUERY_HEADS // KEY_VALUE_HEADS


EPS = 1e-06
ROPE_BASE = 1000000.0
MASKED = -1e30
AXES = ("shard", "replica")
F32, BF16 = jnp.float32, jnp.bfloat16
SCALE = 1.0 / math.sqrt(HEAD_SIZE)
VMEM = 60 << 20
LIGHT = pl.CostEstimate(flops=1, bytes_accessed=1, transcendentals=0)


def pack_layout(lengths):
    ends = jnp.cumsum(lengths)
    starts = ends - lengths
    slots = jnp.arange(PACK_CAPACITY, dtype=jnp.int32)
    segment = jnp.sum((slots[:, None] >= ends[None, :]).astype(jnp.int32), axis=1)
    live = slots < ends[-1]
    labels = jnp.arange(NSEQ, dtype=jnp.int32)
    begin = jnp.sum(jnp.where(segment[:, None] == labels[None, :], starts[None, :], 0), axis=1)
    position = (slots - begin).astype(jnp.float32)
    segids = jnp.where(live, segment, NSEQ + slots)
    freqs = ROPE_BASE ** (-2.0 * jnp.arange(HEAD_SIZE // 2, dtype=jnp.float32) / HEAD_SIZE)
    angle = position[:, None] * freqs[None, :]
    cosine = jnp.concatenate([jnp.cos(angle), jnp.cos(angle)], axis=1)
    sine = jnp.concatenate([jnp.sin(angle), jnp.sin(angle)], axis=1)
    return (segids, cosine, sine, live)


def normalized_rows(value, gain):
    scale_inv = lax.rsqrt(jnp.mean(value * value, axis=-1, keepdims=True) + EPS)
    normed = value * scale_inv
    return (normed * gain, normed, scale_inv)


def norm_back(grad, normed, scale_inv, gain):
    scaled = grad * gain
    grad_in = scale_inv * (scaled - normed * jnp.mean(scaled * normed, axis=-1, keepdims=True))
    grad_gain = jnp.sum((grad * normed).reshape(-1, normed.shape[-1]), axis=0)
    return (grad_in, grad_gain)


def against(grad, matrix):
    return lax.dot_general(
        grad, matrix, (((1,), (1,)), ((), ())), preferred_element_type=jnp.float32
    )


def through(left, grad):
    return lax.dot_general(left, grad, (((0,), (0,)), ((), ())), preferred_element_type=jnp.float32)


class Wires:
    def __init__(self, shards, copies):
        self.shards, self.copies = shards, copies
        bits = shards.bit_length() - 1
        self.masks = [1 << b for b in range(bits)]
        self.top = shards >> 1
        self.team = [1, 4]
        self.far = [m for m in self.masks if m > 4]
        self.spread = [2] + self.far
        self.me = lax.axis_index("shard")
        self.core = lax.axis_index("replica")

    def send(self, value, to):
        pairs = []
        for i in range(self.shards * self.copies):
            goal = to(i // self.copies, i % self.copies)
            if goal is not None:
                pairs.append((i, goal[0] * self.copies + goal[1]))
        return lax.ppermute(value, AXES, pairs)

    def swap(self, value, mask):
        return self.send(value, lambda s, c: (s ^ mask, c))

    def swap_core(self, value):
        return self.send(value, lambda s, c: (s, 1 - c))

    def has(self, mask):
        return (self.me & mask) != 0

    def sharers(self):
        return self.groups(self.team)

    def teams(self):
        return self.groups(self.spread)

    def groups(self, fixed):
        fixed = sum(fixed)
        return [
            [s for s in range(self.shards) if s & fixed == f]
            for f in sorted({s & fixed for s in range(self.shards)})
        ]

    def others(self):
        return self.sharers()[0]


def masks_of(order):
    out = [0]
    for mask in reversed(order):
        out = out + [mask ^ m for m in out]
    return out


def pick_columns(value, block, groups):
    rows, width = value.shape
    places = jnp.stack([jnp.asarray(g, jnp.int32) for group in groups for g in group])
    if block % 128:
        blocks = value.reshape(rows, width // block, block)
        out, at = [], 0
        for group in groups:
            taken = jnp.take(blocks, places[at : at + len(group)], axis=1)
            out.append(taken.reshape(rows, len(group) * block))
            at += len(group)
        return out
    tile = math.gcd(rows, 256)

    def kernel(places_ref, in_ref, *out_refs):
        at = 0
        for group, out_ref in zip(groups, out_refs):
            for i in range(len(group)):
                start = pl.multiple_of(places_ref[at] * block, 128)
                out_ref[:, i * block : (i + 1) * block] = in_ref[:, pl.ds(start, block)]
                at += 1

    widths = [len(group) * block for group in groups]
    return list(
        pl.pallas_call(
            kernel,
            grid_spec=pltpu.PrefetchScalarGridSpec(
                num_scalar_prefetch=1,
                grid=(rows // tile,),
                in_specs=[pl.BlockSpec((tile, width), lambda i, s: (i, 0))],
                out_specs=[pl.BlockSpec((tile, w), lambda i, s: (i, 0)) for w in widths],
            ),
            out_shape=[jax.ShapeDtypeStruct((rows, w), value.dtype) for w in widths],
            compiler_params=pltpu.CompilerParams(vmem_limit_bytes=VMEM),
            cost_estimate=pl.CostEstimate(
                flops=0, bytes_accessed=2 * rows * (width + sum(widths)), transcendentals=0
            ),
            name="pick_columns",
        )(places, value)
    )


def put_columns(values, block, groups):
    rows = values[0].shape[0]
    places = jnp.stack([jnp.asarray(g, jnp.int32) for group in groups for g in group])
    width = block * places.shape[0]
    if block % 128:
        flat = jnp.concatenate([v.astype(F32) for v in values], axis=1)
        blocks = flat.reshape(rows, width // block, block)
        return jnp.zeros_like(blocks).at[:, places].set(blocks).reshape(rows, width)
    tile = math.gcd(rows, 64)

    def kernel(places_ref, *refs):
        out_ref, at = refs[-1], 0
        for group, ref in zip(groups, refs[:-1]):
            for i in range(len(group)):
                start = pl.multiple_of(places_ref[at] * block, 128)
                part = ref[:, i * block : (i + 1) * block]
                out_ref[:, pl.ds(start, block)] = part.astype(F32)
                at += 1

    return pl.pallas_call(
        kernel,
        grid_spec=pltpu.PrefetchScalarGridSpec(
            num_scalar_prefetch=1,
            grid=(rows // tile,),
            in_specs=[pl.BlockSpec((tile, v.shape[1]), lambda i, s: (i, 0)) for v in values],
            out_specs=pl.BlockSpec((tile, width), lambda i, s: (i, 0)),
        ),
        out_shape=jax.ShapeDtypeStruct((rows, width), F32),
        compiler_params=pltpu.CompilerParams(vmem_limit_bytes=VMEM),
        cost_estimate=LIGHT,
        name="put_columns",
    )(places, *values)


def after(value, *others):
    return lax.optimization_barrier((value, others))[0]


class Line:
    def __init__(self):
        self.last = ()

    def take(self, value):
        value = lax.optimization_barrier((value, self.last))[0]
        self.last = value
        return value

    def run(self, fn, *inputs):
        inputs = lax.optimization_barrier((inputs, self.last))[0]
        out = fn(*inputs)
        self.last = out
        return out

    def light(self, fn, *inputs, flags=()):
        return self.run(lambda *v: light(fn, *v, flags=flags), *inputs)


def ordered_pair(bit, own, other):
    return jnp.concatenate([jnp.where(bit, other, own), jnp.where(bit, own, other)], axis=0)


def scatter_sum(wires, keep, order):
    for mask in order:
        half = keep.shape[0] // 2
        got = wires.swap(keep[half:].astype(BF16), mask)
        keep = keep[:half].astype(F32) + got.astype(F32)
    return keep


def team_blocks(wires, half):
    one, two = wires.team
    mine = wires.me & (one | two)
    return [
        [half * wires.shards + ((mine ^ t) | s) for s in wires.others()]
        for t in (0, one, two, one | two)
    ]


def turned(value):
    return pltpu.roll(value, HEAD_SIZE // 2, 1)


def head_forward(raw, gain, cosine, sine):
    scale = lax.rsqrt(jnp.mean(raw * raw, axis=1, keepdims=True) + EPS)
    normed = raw * scale
    v = normed * gain
    return (v * cosine + turned(v) * sine).astype(BF16), normed, scale


def head_back(grad, normed, scale, gain, cosine, sine):
    g = grad * cosine + turned(grad * sine)
    scaled = g * gain
    raw = scale * (scaled - normed * jnp.mean(scaled * normed, axis=1, keepdims=True))
    return raw, jnp.sum(g * normed, axis=0, keepdims=True)


def attend_group(sources, cosine, sine, bias, q_gain, k_gain):
    tokens = sources[0][0].shape[0]
    packs = tokens // PACK_CAPACITY
    width = (GROUPS + 2) * HEAD_SIZE
    counts = [len(pieces) for _, pieces, _ in sources]
    columns = [c for _, _, c in sources]
    n_in = len(sources) + sum(counts)

    def kernel(*refs):
        cos_ref, sin_ref, bias_ref, qg_ref, kg_ref, attn_ref, mixed_ref = refs[n_in:]
        at, to = 0, 0
        for count, (start, stop) in zip(counts, columns):
            x_ref, w_refs = refs[at], refs[at + 1 : at + 1 + count]
            at += 1 + count
            depth = w_refs[0].shape[0]
            part = jnp.zeros((tokens, stop - start), F32)
            for i, w_ref in enumerate(w_refs):
                part += jnp.dot(
                    x_ref[:, i * depth : (i + 1) * depth], w_ref[:, start:stop],
                    preferred_element_type=F32,
                )
            mixed_ref[:, to : to + stop - start] = part
            to += stop - start
        for p in range(packs):
            at = slice(p * PACK_CAPACITY, (p + 1) * PACK_CAPACITY)
            cosine, sine, bias = cos_ref[at], sin_ref[at], bias_ref[at]
            head = lambda j: mixed_ref[at, j * HEAD_SIZE : (j + 1) * HEAD_SIZE]
            key, _, _ = head_forward(head(GROUPS), kg_ref[...], cosine, sine)
            value = head(GROUPS + 1).astype(BF16)
            for j in range(GROUPS):
                query, _, _ = head_forward(head(j), qg_ref[...], cosine, sine)
                scores = against(query, key) * SCALE + bias
                expd = jnp.exp(scores - jnp.max(scores, axis=1, keepdims=True))
                probs = expd / jnp.sum(expd, axis=1, keepdims=True)
                attn = jnp.dot(probs.astype(BF16), value, preferred_element_type=F32)
                attn_ref[at, j * HEAD_SIZE : (j + 1) * HEAD_SIZE] = attn.astype(BF16)

    d = sources[0][0].shape[1]
    return pl.pallas_call(
        kernel,
        out_shape=[
            jax.ShapeDtypeStruct((tokens, GROUPS * HEAD_SIZE), BF16),
            jax.ShapeDtypeStruct((tokens, width), F32),
        ],
        compiler_params=pltpu.CompilerParams(vmem_limit_bytes=VMEM),
        cost_estimate=LIGHT,
        name="attend_group",
    )(
        *[v for x, pieces, _ in sources for v in (x, *pieces)],
        cosine, sine, bias, q_gain, k_gain,
    )


def attend_group_back(mixed, grad, cosine, sine, bias, q_gain, k_gain):
    tokens, width = mixed.shape
    packs = tokens // PACK_CAPACITY

    def kernel(mixed_ref, grad_ref, cos_ref, sin_ref, bias_ref, qg_ref, kg_ref, out_ref, gain_ref):
        q_gain, k_gain = qg_ref[...], kg_ref[...]
        q_sum = jnp.zeros((1, HEAD_SIZE), F32)
        k_sum = jnp.zeros((1, HEAD_SIZE), F32)
        for p in range(packs):
            at = slice(p * PACK_CAPACITY, (p + 1) * PACK_CAPACITY)
            cosine, sine, bias = cos_ref[at], sin_ref[at], bias_ref[at]
            head = lambda j: mixed_ref[at, j * HEAD_SIZE : (j + 1) * HEAD_SIZE]
            key, key_normed, key_scale = head_forward(head(GROUPS), k_gain, cosine, sine)
            value = head(GROUPS + 1).astype(BF16)
            grad_key = jnp.zeros((PACK_CAPACITY, HEAD_SIZE), F32)
            grad_value = jnp.zeros((PACK_CAPACITY, HEAD_SIZE), F32)
            for j in range(GROUPS):
                cols = slice(j * HEAD_SIZE, (j + 1) * HEAD_SIZE)
                query, normed, scale = head_forward(head(j), q_gain, cosine, sine)
                g = grad_ref[at, cols]
                scores = against(query, key) * SCALE + bias
                expd = jnp.exp(scores - jnp.max(scores, axis=1, keepdims=True))
                probs = expd / jnp.sum(expd, axis=1, keepdims=True)
                dprobs = against(g, value)
                inner = jnp.sum(probs * dprobs, axis=1, keepdims=True)
                grad_scores = (probs * (dprobs - inner)).astype(BF16)
                grad_query = jnp.dot(grad_scores, key, preferred_element_type=F32) * SCALE
                grad_key += through(grad_scores, query)
                grad_value += through(probs.astype(BF16), g)
                raw, gain = head_back(grad_query, normed, scale, q_gain, cosine, sine)
                out_ref[at, cols] = raw.astype(BF16)
                q_sum += gain
            raw, gain = head_back(grad_key * SCALE, key_normed, key_scale, k_gain, cosine, sine)
            k_sum += gain
            out_ref[at, GROUPS * HEAD_SIZE : (GROUPS + 1) * HEAD_SIZE] = raw.astype(BF16)
            out_ref[at, (GROUPS + 1) * HEAD_SIZE :] = grad_value.astype(BF16)
        gain_ref[...] = jnp.concatenate([q_sum, k_sum] + [jnp.zeros_like(q_sum)] * 6, axis=0)

    return pl.pallas_call(
        kernel,
        out_shape=[
            jax.ShapeDtypeStruct((tokens, width), BF16),
            jax.ShapeDtypeStruct((8, HEAD_SIZE), F32),
        ],
        compiler_params=pltpu.CompilerParams(vmem_limit_bytes=VMEM),
        cost_estimate=LIGHT,
        name="attend_group_back",
    )(mixed, grad, cosine, sine, bias, q_gain, k_gain)


def spread_back(grads, weights, groups, block, dtype, parts, by_rows=False):
    tokens = grads[0].shape[0]
    width = sum(w.shape[0] for w in weights[0])
    places = jnp.stack([jnp.asarray(g, jnp.int32) for group in groups for g in group])
    if block % 128:
        total = 0.0
        for grad, pieces, group in zip(grads, weights, groups):
            part = jnp.concatenate([against(grad, w) for w in pieces], axis=1)
            total = total + put_columns([part], block, [group])
        return jnp.split(total.astype(dtype), parts, axis=0 if by_rows else 1)
    flat = [w for pieces in weights for w in pieces]
    shape = (tokens // parts, width) if by_rows else (tokens, width // parts)

    def kernel(places_ref, *refs):
        grad_refs, refs = refs[: len(grads)], refs[len(grads) :]
        out_ref, at, k = refs[-1], 0, 0
        out_refs = refs[-1 - parts : -1]
        for gi, grad_ref in enumerate(grad_refs):
            for _ in weights[gi]:
                part = against(grad_ref[...], refs[k][...])
                for b in range(part.shape[1] // block):
                    start = pl.multiple_of(places_ref[at] * block, 128)
                    cols = pl.ds(start, block)
                    new = part[:, b * block : (b + 1) * block]
                    out_ref[:, cols] = new if gi == 0 else out_ref[:, cols] + new
                    at += 1
                k += 1
        for i, ref in enumerate(out_refs):
            size = ref.shape[0] if by_rows else ref.shape[1]
            part = slice(i * size, (i + 1) * size)
            ref[...] = (out_ref[part, :] if by_rows else out_ref[:, part]).astype(dtype)

    whole = lambda v: pl.BlockSpec(v.shape, lambda i, s: (0, 0))
    return pl.pallas_call(
        kernel,
        grid_spec=pltpu.PrefetchScalarGridSpec(
            num_scalar_prefetch=1,
            grid=(1,),
            in_specs=[whole(v) for v in grads] + [whole(w) for w in flat],
            out_specs=[pl.BlockSpec(shape, lambda i, s: (0, 0))] * parts,
            scratch_shapes=[pltpu.VMEM((tokens, width), F32)],
        ),
        out_shape=[jax.ShapeDtypeStruct(shape, dtype)] * parts,
        compiler_params=pltpu.CompilerParams(vmem_limit_bytes=VMEM),
        cost_estimate=LIGHT,
        name="spread_back",
    )(places, *grads, *flat)


def feed_forward(second, own, other, grad_low, down_own, down_other, core):
    rows, d = second[0].shape
    n = len(second)
    tokens = n * rows
    units = down_own.shape[0]
    tile, half = 384, d // 2

    def kernel(core_ref, *refs):
        x_refs, go_refs, gx_refs = refs[:n], refs[n : 2 * n], refs[2 * n : 3 * n]
        own_ref, other_ref, do_ref, dx_ref, hidden_ref, out_own_ref, out_other_ref = refs[3 * n :]
        first = core_ref[0] == 0
        for r in range(n):
            at = slice(r * rows, (r + 1) * rows)
            x = x_refs[r][...]
            a = jnp.dot(x, own_ref[...], preferred_element_type=F32)
            b = jnp.dot(x, other_ref[...], preferred_element_type=F32)
            gate, upward = jnp.where(first, a, b), jnp.where(first, b, a)
            sigma = jax.nn.sigmoid(gate)
            silu = gate * sigma
            hidden_ref[at, :] = (silu * upward).astype(BF16)
            grad = against(go_refs[r][...], do_ref[...]) + against(gx_refs[r][...], dx_ref[...])
            grad_gate = grad * upward * sigma * (1.0 + gate * (1.0 - sigma))
            grad_up = grad * silu
            out_own_ref[at, :] = jnp.where(first, grad_gate, grad_up).astype(BF16)
            out_other_ref[at, :] = jnp.where(first, grad_up, grad_gate).astype(BF16)

    once = pl.Buffered(1)
    in_specs = [pl.BlockSpec((rows, d), lambda j, s: (0, 0), pipeline_mode=once)] * n
    in_specs += [pl.BlockSpec((rows, half), lambda j, s: (0, s[0]), pipeline_mode=once)] * n
    in_specs += [pl.BlockSpec((rows, half), lambda j, s: (0, 1 - s[0]), pipeline_mode=once)] * n
    in_specs += [pl.BlockSpec((d, tile), lambda j, s: (0, j))] * 2
    in_specs += [pl.BlockSpec((tile, half), lambda j, s: (j, 0))] * 2
    return pl.pallas_call(
        kernel,
        grid_spec=pltpu.PrefetchScalarGridSpec(
            num_scalar_prefetch=1,
            grid=(units // tile,),
            in_specs=in_specs,
            out_specs=[pl.BlockSpec((tokens, tile), lambda j, s: (0, j))] * 3,
        ),
        out_shape=[jax.ShapeDtypeStruct((tokens, units), BF16)] * 3,
        compiler_params=pltpu.CompilerParams(vmem_limit_bytes=VMEM),
        cost_estimate=LIGHT,
        name="feed_forward",
    )(core.reshape(1), *second, *grad_low, *grad_low, own, other, down_own, down_other)


def feed_forward_back(grad_own, grad_other, own, other, places, block, n):
    tokens, units = grad_own.shape
    d = own.shape[0]
    rows = tokens // n
    if block % 128:
        part = against(grad_own, own) + against(grad_other, other)
        part = put_columns([part], block, [places]).astype(BF16)
        return [part[i * rows : (i + 1) * rows] for i in range(n)]
    width = 512

    def kernel(go_ref, gx_ref, own_ref, other_ref, *out_refs):
        for at in range(0, d, width):
            part = against(go_ref[...], own_ref[at : at + width, :])
            part += against(gx_ref[...], other_ref[at : at + width, :])
            part = part.astype(BF16)
            for b in range(width // block):
                to = places[at // block + b] * block
                for i in range(n):

                    @pl.when(pl.program_id(0) == (n - 1 - i) // 2)
                    def _(i=i, b=b, to=to):
                        row = (i % 2) * rows
                        out_refs[i][:, to : to + block] = part[
                            row : row + rows, b * block : (b + 1) * block
                        ]

    return pl.pallas_call(
        kernel,
        grid=(n // 2,),
        in_specs=[pl.BlockSpec((2 * rows, units), lambda i: (n // 2 - 1 - i, 0))] * 2
        + [pl.BlockSpec(own.shape, lambda i: (0, 0), pipeline_mode=pl.Buffered(1))] * 2,
        out_specs=[pl.BlockSpec((rows, d), lambda i: (0, 0))] * n,
        out_shape=[jax.ShapeDtypeStruct((rows, d), BF16)] * n,
        compiler_params=pltpu.CompilerParams(vmem_limit_bytes=VMEM),
        cost_estimate=LIGHT,
        name="feed_forward_back",
    )(grad_own, grad_other, own, other)


def weight_grad(lefts, tile, rights, column, width, added=None, split=False):
    units = lefts[0].shape[1]
    n, m = len(lefts), len(rights)
    steps = units // tile
    row_of = lambda vs, at: next(
        (i, at - sum(v.shape[0] for v in vs[:i]))
        for i in range(len(vs))
        if at < sum(v.shape[0] for v in vs[: i + 1])
    )
    tokens = sum(v.shape[0] for v in lefts)
    piece = min(v.shape[0] for v in [*lefts, *rights])

    def kernel(column_ref, *refs):
        left_refs, right_refs = refs[:n], refs[n : n + m]
        total = None
        for at in range(0, tokens, piece):
            (i, a), (j, b) = row_of(lefts, at), row_of(rights, at)
            part = through(left_refs[i][a : a + piece, :], right_refs[j][b : b + piece, :])
            total = part if total is None else total + part
        if added is not None:
            total += refs[n + m][...].astype(F32)
        if not split:
            refs[-1][...] = total.astype(BF16)
        else:

            @pl.when(pl.program_id(0) < steps // 2)
            def _():
                refs[-2][...] = total.astype(BF16)

            @pl.when(pl.program_id(0) >= steps // 2)
            def _():
                refs[-1][...] = total.astype(BF16)

    extra = [] if added is None else [added]
    once = pl.Buffered(1)
    half = steps // 2
    if split:
        out_specs = [
            pl.BlockSpec((tile, width), lambda i, s: (jnp.minimum(i, half - 1), 0)),
            pl.BlockSpec((tile, width), lambda i, s: (jnp.maximum(i - half, 0), 0)),
        ]
        out_shape = [jax.ShapeDtypeStruct((units // 2, width), BF16)] * 2
    else:
        out_specs = pl.BlockSpec((tile, width), lambda i, s: (i, 0))
        out_shape = jax.ShapeDtypeStruct((units, width), BF16)
    return pl.pallas_call(
        kernel,
        grid_spec=pltpu.PrefetchScalarGridSpec(
            num_scalar_prefetch=1,
            grid=(steps,),
            in_specs=[pl.BlockSpec((v.shape[0], tile), lambda i, s: (0, i)) for v in lefts]
            + [
                pl.BlockSpec((v.shape[0], width), lambda i, s: (0, s[0]), pipeline_mode=once)
                for v in rights
            ]
            + [pl.BlockSpec((tile, width), lambda i, s: (i, 0))] * len(extra),
            out_specs=out_specs,
        ),
        out_shape=out_shape,
        compiler_params=pltpu.CompilerParams(vmem_limit_bytes=VMEM),
        cost_estimate=LIGHT,
        name="weight_grad",
    )(jnp.asarray(column, jnp.int32).reshape(1), *lefts, *rights, *extra)


def down_project(hidden, own, other):
    tokens, units = hidden.shape
    half = own.shape[1]
    n = 4
    rows = tokens // n

    def kernel(hidden_ref, own_ref, other_ref, *out_refs):
        for r, out_ref in enumerate(out_refs):

            @pl.when(pl.program_id(0) == r)
            def _(out_ref=out_ref):
                for i, ref in enumerate((own_ref, other_ref)):
                    part = jnp.dot(hidden_ref[...], ref[...], preferred_element_type=F32)
                    out_ref[:, i * half : (i + 1) * half] = part.astype(BF16)

    once = pl.Buffered(1)
    return pl.pallas_call(
        kernel,
        grid=(n,),
        in_specs=[pl.BlockSpec((rows, units), lambda i: (i, 0))]
        + [pl.BlockSpec((units, half), lambda i: (0, 0), pipeline_mode=once)] * 2,
        out_specs=[pl.BlockSpec((rows, 2 * half), lambda i: (0, 0))] * n,
        out_shape=[jax.ShapeDtypeStruct((rows, 2 * half), BF16)] * n,
        compiler_params=pltpu.CompilerParams(vmem_limit_bytes=VMEM),
        cost_estimate=LIGHT,
        name="down_project",
    )(hidden, own, other)


def light(fn, *args, flags=()):
    flat, tree = jax.tree.flatten(args)
    n = len(flags)
    shapes = jax.eval_shape(lambda *v: fn(*[jnp.bool_(True)] * n, *v), *args)
    out_flat, out_tree = jax.tree.flatten(shapes)

    def kernel(*refs):
        flag_ref, refs = refs[0], refs[1:]
        values = jax.tree.unflatten(tree, [r[...] for r in refs[: len(flat)]])
        out = fn(*[flag_ref[i] != 0 for i in range(n)], *values)
        for ref, value in zip(refs[len(flat) :], jax.tree.leaves(out)):
            ref[...] = value

    bits = jnp.stack([jnp.asarray(f, jnp.int32) for f in (*flags, True)])
    whole = lambda v: pl.BlockSpec(v.shape, lambda i, s, r=len(v.shape): (0,) * r)
    out = pl.pallas_call(
        kernel,
        grid_spec=pltpu.PrefetchScalarGridSpec(
            num_scalar_prefetch=1,
            grid=(1,),
            in_specs=[whole(v) for v in flat],
            out_specs=[whole(v) for v in out_flat],
        ),
        out_shape=[jax.ShapeDtypeStruct(v.shape, v.dtype) for v in out_flat],
        compiler_params=pltpu.CompilerParams(vmem_limit_bytes=VMEM),
        cost_estimate=LIGHT,
        name="light",
    )(bits, *flat)
    return jax.tree.unflatten(out_tree, out)


def tables(lengths):
    segids, cosine, sine, live = pack_layout(lengths)
    slots = jnp.arange(PACK_CAPACITY, dtype=jnp.int32)
    allowed = (segids[:, None] == segids[None, :]) & (slots[:, None] >= slots[None, :])
    half = HEAD_SIZE // 2
    sine = jnp.concatenate([-sine[:, :half], sine[:, half:]], axis=1)
    return cosine, sine, jnp.where(allowed, 0.0, MASKED).astype(F32), live


def on_device(
    shards,
    copies,
    tokens,
    seq_lengths,
    in_gain,
    q_gain,
    key_norm_gain,
    post_gain,
    w_qkv,
    w_out,
    w_gate_up,
    w_down,
    cotangent,
):
    wires = Wires(shards, copies)
    me, core, top = wires.me, wires.core, wires.top
    first_core = core == 0
    rows = w_qkv.shape[0]
    d = in_gain.shape[0]
    half = d // 2
    by_core = lambda own, other: (jnp.where(first_core, own, other), jnp.where(first_core, other, own))
    ordered = lambda own, other: jnp.concatenate(by_core(own, other), axis=-1)
    dot = lambda a, b: jnp.dot(a, b, preferred_element_type=F32)
    through_low = lambda a, b: through(a, b).astype(BF16)
    both_packs = lambda v: jnp.concatenate([v, wires.swap_core(v)], axis=0)

    per_core = KEY_VALUE_HEADS // 2
    one, two = wires.team
    x, y, z = 1, 2, 4
    line = Line()
    stack = lambda *parts: jnp.concatenate(parts, axis=0)
    swap, swap_core = wires.swap, wires.swap_core
    low = lambda v: v.astype(BF16)
    wide = lambda v: v.astype(F32)

    def halves(v):
        n = v.shape[0] // 2
        return v[:n], v[n:]

    def head_blocks(core):
        return [
            [GROUPS * (per_core * core + g) + j for j in range(GROUPS)]
            + [QUERY_HEADS + per_core * core + g, QUERY_HEADS + KEY_VALUE_HEADS + per_core * core + g]
            for g in range(per_core)
        ]

    def parcels(core):
        by = head_blocks(core)
        return [by[0] + by[3][:GROUPS], by[1] + by[3][GROUPS:], by[2]]

    qkv_orders = [wires.far + o for o in ([z, x, y], [y, z, x], [x, y, z])]
    widths = [len(p) * HEAD_SIZE for p in parcels(core)]
    starts = [sum(widths[:i]) for i in range(len(widths))]

    lengths_got = swap_core(seq_lengths.astype(F32))
    gu_parts = line.run(
        lambda w: pick_columns(w, FF // shards, team_blocks(wires, core)), w_gate_up
    )
    gu_got = [swap(p, t) for p, t in zip(gu_parts[1:], (one, two, one | two))]
    (qkv_rows,) = line.run(
        lambda w: pick_columns(w, HEAD_SIZE, [sum(parcels(core), [])]), w_qkv
    )
    qkv_got = swap(qkv_rows, wires.far[0])
    lengths_got = line.take(lengths_got)
    row = lambda v: v.reshape(1, -1)
    first_own = line.light(
        lambda v, g: low(normalized_rows(wide(v), g)[0]), tokens, row(in_gain)
    )
    first_other = swap_core(first_own)
    at_home = wires.has(top) == (core == 1)
    away_to = lambda s, c: (s ^ top, c) if (s & top != 0) == (c == 1) else None
    cosine, sine, bias, live = tables(seq_lengths[0])
    lengths_other = lengths_got[0].astype(jnp.int32)
    packs = [
        jnp.concatenate(pair, axis=0)
        for pair in zip((cosine, sine, bias), tables(lengths_other)[:3])
    ]
    gains = [q_gain.reshape(1, -1), key_norm_gain.reshape(1, -1)]
    live = live[:, None].astype(F32)
    packs, live = line.run(lambda *v: v, packs, live)
    grad_low = line.light(lambda v, k: low(wide(v) * k), cotangent, live)
    (down_half,) = line.run(lambda w: pick_columns(w, half, [[core]]), w_down)
    gu_got, qkv_got, first_other = line.take((gu_got, qkv_got, first_other))

    def team_rows(has_one, has_two, own, by_one, by_two, by_both):
        near = ordered_pair(has_one, own, by_one)
        return ordered_pair(has_two, near, ordered_pair(has_one, by_two, by_both))

    team_flags = (wires.has(one), wires.has(two))
    for mask in wires.far:
        got = qkv_got if mask == wires.far[0] else line.take(swap(qkv_rows, mask))
        qkv_rows = line.light(stack, qkv_rows, got)
    legs = line.light(lambda v: [v[:, at : at + w] for at, w in zip(starts, widths)], qkv_rows)
    leg = len(wires.far)
    got = [swap(v, o[leg]) for v, o in zip(legs, qkv_orders)]
    away = wires.send(w_out, away_to)
    down_y = swap(line.take(down_half), y)
    gu_rows = line.light(
        lambda *v: halves(team_rows(*v)), gu_parts[0], *gu_got, flags=team_flags
    )
    gu_a, gu_b = gu_rows

    def spread_far(v):
        out = [v]
        for mask in wires.far:
            out = out + [swap(p, mask) for p in out]
        return out

    block_places = [[me ^ m for m in masks_of(order[::-1])] for order in qkv_orders]
    first_low = line.light(stack, first_own, first_other)
    first_moved = line.run(lambda v: pick_columns(v, rows, block_places), first_low)
    join = lambda a, b: [stack(v, g) for v, g in zip(a, b)]
    legs = line.light(join, legs, line.take(got))
    got = [swap(v, o[leg + 1]) for v, o in zip(legs, qkv_orders)]
    gu_a = spread_far(gu_a)
    got, away, down_y = line.take((got, away, down_y))
    legs = line.light(join, legs, got)
    got = [swap(v, o[leg + 2]) for v, o in zip(legs, qkv_orders)]
    out_legs = line.light(
        lambda home, v, w: jnp.where(home, w, v), away, w_out, flags=(at_home,)
    )
    got, gu_a = line.take((got, gu_a))
    qkv = [[v, g] for v, g in zip(legs, got)]

    out_masks = [m for m in wires.far if m != top]
    out_orders = [out_masks + o for o in ([z, x, y], [z, y, x])]
    for mask in out_masks:
        out_legs = line.light(stack, out_legs, line.take(swap(out_legs, mask)))
    out_legs, grad_low = line.take((out_legs, grad_low))
    got = swap(out_legs, z)
    grad_low_one = swap(grad_low, one)
    grad_low_two = swap(grad_low, two)
    gu_a_y = [swap(gu_a[0], y)]
    gu_b = spread_far(line.take(gu_b))
    attn, mixed = [], []

    def attend(g):
        if g < 3:
            sources = [(first_moved[g], qkv[g], (0, (GROUPS + 2) * HEAD_SIZE))]
        else:
            at = (GROUPS + 2) * HEAD_SIZE
            sources = [
                (first_moved[i], qkv[i], (at, at + GROUPS * HEAD_SIZE)) for i in range(2)
            ]
        out = line.run(
            lambda cosine: attend_group(sources, cosine, *packs[1:], *gains), packs[0]
        )
        attn.append(out[0])
        mixed.append(out[1])

    attend(0)
    attend(1)
    got, grad_low_one, gu_a_y[0] = line.take((got, grad_low_one, gu_a_y[0]))
    out_legs = line.light(
        lambda v, g: [stack(v, g)[:, i * half : (i + 1) * half] for i in range(2)], out_legs, got
    )
    got = [swap(v, o[-2]) for v, o in zip(out_legs, out_orders)]
    gu_b_y = [swap(line.take(gu_b[0]), y)]
    attend(2)
    attend(3)
    gu_b = line.take(gu_b)
    down_far = spread_far(line.take(down_half))
    got, grad_low_two, gu_b_y[0] = line.take((got, grad_low_two, gu_b_y[0]))
    out_legs = line.light(join, out_legs, got)
    got = [swap(v, o[-1]) for v, o in zip(out_legs, out_orders)]
    gu_a_y = gu_a_y + [swap(v, y) for v in line.take(gu_a[1:])]
    grad_low_both = swap(line.take(grad_low_one), two)
    below = top - 1
    out_places = [[(me & below) ^ m for m in masks_of(o[::-1])] for o in out_orders]
    attn = line.light(lambda *v: jnp.concatenate(v, axis=1), *attn)
    attn_moved = line.run(lambda v: pick_columns(v, rows, out_places), attn)
    got, grad_low_both, down_far = line.take((got, grad_low_both, down_far))
    out_w = [[v, g] for v, g in zip(out_legs, got)]

    def project_out(moved, weights):
        parts = []
        for v, w in zip(moved, weights):
            depth = w[0].shape[0]
            parts.append(sum(dot(v[:, i * depth : (i + 1) * depth], p) for i, p in enumerate(w)))
        part = jnp.concatenate(parts, axis=1)
        return part[:PACK_CAPACITY], low(part[PACK_CAPACITY:])

    out_part, out_send = line.light(project_out, attn_moved, out_w)
    out_got = line.take(swap_core(out_send))
    columns = [f | t for f in wires.sharers()[0] for t in (0, one, two, one | two)]

    def to_second(v, part, got, gain):
        middle = wide(v) + (part + wide(got))
        second = low(normalized_rows(middle, gain)[0])
        return middle, jnp.concatenate([second[:, c * rows : (c + 1) * rows] for c in columns], axis=1)

    middle, second_low = line.light(to_second, tokens, out_part, out_got, row(post_gain))

    second_two = swap(second_low, two)
    second_one = swap(second_low, one)
    gu_b_y = gu_b_y + [swap(v, y) for v in gu_b[1:]]
    down_far_y = [down_y] + [swap(v, y) for v in down_far[1:]]
    gu_a_y, gu_b_y, second_two = line.take((gu_a_y, gu_b_y, second_two))
    second_both = swap(second_two, one)
    second_one, second_both, down_far_y = line.take((second_one, second_both, down_far_y))
    order_flags = [wires.has(y)] + [wires.has(mask) for mask in wires.far]

    def in_order(*v):
        flags, (near, by_y) = v[: len(order_flags)], v[len(order_flags) :]
        rows_of = [ordered_pair(flags[0], a, b) for a, b in zip(near, by_y)]
        for flag in flags[1:]:
            rows_of = [ordered_pair(flag, a, b) for a, b in zip(rows_of[::2], rows_of[1::2])]
        return rows_of[0]

    gu_own = line.light(
        lambda *v: in_order(
            *v[: len(order_flags)],
            *[
                [jnp.concatenate(pair, axis=0) for pair in zip(a, b)]
                for a, b in (v[-4:-2], v[-2:])
            ],
        ),
        gu_a, gu_b, gu_a_y, gu_b_y, flags=order_flags,
    )
    gu_other = swap_core(gu_own)
    down_own = line.light(in_order, down_far, down_far_y, flags=order_flags)
    down_other = swap_core(down_own)
    gu_other, down_other = line.take((gu_other, down_other))

    second_team = [second_low, second_two, second_one, second_both]
    grad_low_team = [grad_low, grad_low_two, grad_low_one, grad_low_both]
    hidden_low, grad_own, grad_other = line.run(
        lambda v, g: feed_forward(v, gu_own, gu_other, g, down_own, down_other, core),
        second_team, grad_low_team,
    )
    def down_blocks(has_y, v):
        n = v.shape[0] // (shards // 4)
        by = [v[i * n : (i + 1) * n] for i in range(shards // 4)]
        low_y, high_y = jnp.concatenate(by[::2], axis=0), jnp.concatenate(by[1::2], axis=0)
        return jnp.where(has_y, high_y, low_y), jnp.where(has_y, low_y, high_y)

    def far_blocks(has_far, mine, got):
        one_half, other_half = halves(wide(mine) + wide(got))
        return (
            jnp.where(has_far, other_half, one_half),
            low(jnp.where(has_far, one_half, other_half)),
        )

    units = hidden_low.shape[1]
    gu_sent = swap_core(
        line.run(lambda g: weight_grad(second_team, 512, [g], 0, units), grad_other)
    )
    down_sent = swap_core(
        line.run(lambda h: weight_grad([h], 384, grad_low_team, 1 - core, half), hidden_low)
    )
    share_own, share_two, share_one, share_both = line.run(
        lambda a, b: feed_forward_back(a, b, gu_own, gu_other, columns, rows, 4),
        grad_own, grad_other,
    )
    got_two = swap(share_both, one)

    gu_sent, down_sent = line.take((gu_sent, down_sent))
    gu_keep = line.run(
        lambda g, sent: weight_grad(second_team, 512, [g], 0, units, sent), grad_own, gu_sent
    )
    gu_keep = line.light(
        lambda has_y, v: down_blocks(has_y, v), gu_keep, flags=(wires.has(y),)
    )
    gu_got = swap(gu_keep[1], y)
    got_two = line.take(got_two)
    got_last = swap(line.light(lambda a, b: low(wide(a) + wide(b)), share_two, got_two), two)
    got_own = swap(line.take(share_one), one)
    down_keep = line.run(
        lambda h, sent: weight_grad([h], 384, grad_low_team, core, half, sent), hidden_low, down_sent
    )
    down_keep = line.light(
        lambda has_y, v: down_blocks(has_y, v), down_keep, flags=(wires.has(y),)
    )
    down_got = swap(down_keep[1], y)
    part_own, part_two, part_one, part_both = line.run(
        lambda h: down_project(h, down_own, down_other), hidden_low
    )
    got_own, got_last = line.take((got_own, got_last))

    def norm_gradient(parts, v, gain):
        _, normed, scale = normalized_rows(v, gain)
        grad = sum(wide(p) for p in parts)
        scaled = grad * gain
        mean = jnp.mean(scaled * normed, axis=-1, keepdims=True)
        return scale * (scaled - normed * mean), jnp.sum(grad * normed, axis=0, keepdims=True)

    def to_middle(parts, v, gain, cotangent, live):
        norm_part, gain_part = norm_gradient(parts, v, gain)
        grad = wide(cotangent) * live + norm_part
        return grad, low(grad), gain_part

    grad_middle, grad_middle_own, post_gain_grad = line.light(
        to_middle, (share_own, got_own, got_last), middle, row(post_gain), cotangent, live
    )
    grad_middle_other = swap_core(grad_middle_own)
    part_got_two = swap(line.take(part_both), one)
    grad_middle_low, *out_cols = line.light(
        lambda a, b: (stack(a, b), stack(a, b)[:, :half], stack(a, b)[:, half:]),
        grad_middle_own, line.take(grad_middle_other),
    )
    grad_attn = line.run(
        lambda *cols: spread_back(cols, out_w, out_places, rows, BF16, per_core), *out_cols
    )
    n_out = attn_moved[0].shape[1]
    out_back = [x, z, y] + out_masks[::-1]
    attn_back = line.run(
        lambda v: pick_columns(v, rows, [[(me & below) ^ m for m in masks_of(out_back)]])[0], attn
    )
    grad_mixed, gain_grads = {}, []

    def attend_back(g):
        got = line.run(
            lambda v: attend_group_back(
                mixed[g],
                v[g],
                *packs,
                *gains,
            ),
            grad_attn,
        )
        grad_mixed[g] = got[0]
        gain_grads.append(got[1])

    q_width = GROUPS * HEAD_SIZE
    qkv_back = [o[::-1] for o in qkv_orders]

    def next_step(keep, got):
        mine, away = halves(wide(keep) + wide(got))
        return mine, low(away)

    def far_step(keep, got):
        for mask in wires.far[::-1]:
            keep, away = line.light(far_blocks, keep, got, flags=(wires.has(mask),))
            got = swap(away, mask)
            if mask != wires.far[0]:
                got = line.take(got)
        return keep, got

    def parcel_back(g, *extra):
        parcel = grad_mixed[g]
        if extra:
            parcel = line.light(lambda *v: jnp.concatenate(v, axis=1), parcel, *extra)
        keep = line.run(
            lambda v, p: weight_grad([v], 512, [p], 0, p.shape[1], split=True),
            first_moved[g], parcel,
        )
        return parcel, keep, swap(keep[1], qkv_back[g][0])

    def add_step(keep, got, mask):
        keep = line.light(next_step, keep[0], line.take(got))
        return keep, swap(keep[1], mask)

    attend_back(3)
    last_q, last_kv = line.light(lambda v: (v[:, :q_width], v[:, q_width:]), grad_mixed[3])
    attend_back(1)
    part_got_two = line.take(part_got_two)
    part_got_last = swap(line.light(lambda a, b: low(wide(a) + wide(b)), part_two, part_got_two), two)
    part_got_own = swap(line.take(part_one), one)
    parcels_back = {1: parcel_back(1, last_kv)}
    attend_back(2)
    parcels_back[2] = parcel_back(2)
    out_keep = line.run(
        lambda v: weight_grad([v], n_out // 4, [grad_middle_low], 0, d, split=True), attn_back
    )
    out_got = swap(out_keep[1], out_back[0])
    attend_back(0)
    part_got_own, part_got_last = line.take((part_got_own, part_got_last))

    def to_result(own_first, m, parts):
        total = sum(wide(v) for v in parts)
        a, b = total[:, :half], total[:, half:]
        columns = [jnp.where(own_first, a, b), jnp.where(own_first, b, a)]
        return low(m + jnp.concatenate(columns, axis=1))

    result = line.light(
        to_result, middle, (part_own, part_got_own, part_got_last), flags=(first_core,)
    )
    keep_2, got_2 = add_step(parcels_back[2][1], parcels_back[2][2], qkv_back[2][1])
    parcels_back[2] = (parcels_back[2][0], keep_2, got_2)
    gu_got, down_got = line.take((gu_got, down_got))
    gu_mine, gu_far_got = far_step(gu_keep[0], gu_got)
    parcels_back[0] = parcel_back(0, last_q)
    grad_parcels = [parcels_back[g][0] for g in range(3)]
    keeps = [parcels_back[g][1] for g in range(3)]
    gots = [parcels_back[g][2] for g in range(3)]
    keeps[1], gots[1] = add_step(keeps[1], gots[1], qkv_back[1][1])
    grad_first_part = line.run(
        lambda *g: spread_back(g, qkv, block_places, rows, BF16, 2, True), *grad_parcels
    )
    keeps[0], gots[0] = add_step(keeps[0], gots[0], qkv_back[0][1])
    keeps[1], gots[1] = add_step(keeps[1], gots[1], qkv_back[1][2])
    keeps[2], gots[2] = add_step(keeps[2], gots[2], qkv_back[2][2])
    out_keep, out_got = add_step(out_keep, out_got, out_back[1])
    gu_far_got = line.take(gu_far_got)
    gu_half = line.light(lambda a, b: low(a + wide(b)), gu_mine, gu_far_got)
    down_mine, down_got = far_step(down_keep[0], down_got)
    first_got = line.take(swap_core(grad_first_part[1]))

    def to_tokens(parts, v, gain, grad):
        norm_part, gain_part = norm_gradient(parts, wide(v), gain)
        return low(grad + norm_part), gain_part

    grad_tokens, in_gain_grad = line.light(
        to_tokens, (grad_first_part[0], first_got), tokens, row(in_gain), grad_middle
    )
    sums = jnp.concatenate(
        [
            in_gain_grad.reshape(-1, HEAD_SIZE),
            post_gain_grad.reshape(-1, HEAD_SIZE),
            sum(gain_grads),
        ]
    )
    keeps[0], gots[0] = add_step(keeps[0], gots[0], qkv_back[0][2])
    def return_rows(has_one, has_two, v):
        by = [v[i * rows : (i + 1) * rows] for i in range(4)]
        near = [jnp.where(has_two, by[i + 2], by[i]) for i in range(2)]
        away = [jnp.where(has_two, by[i], by[i + 2]) for i in range(2)]
        pick = lambda pair: [
            jnp.where(has_one, pair[1], pair[0]), jnp.where(has_one, pair[0], pair[1])
        ]
        return pick(near) + pick(away)

    back_to = lambda s, c: (s ^ top, c) if (s & top != 0) != (c == 1) else None
    sums = sums + line.take(swap_core(sums))
    sums_got = swap(sums, wires.masks[0])
    out_keep, out_got = add_step(out_keep, out_got, out_back[2])
    sums = sums + line.take(sums_got)
    sums_got = swap(sums, wires.masks[1])
    gots, out_got, sums_got = line.take((gots, out_got, sums_got))
    sums = sums + sums_got
    cut = lambda v: (halves(v)[0], low(halves(v)[1]))
    mine, away = line.light(
        lambda a, b: cut(jnp.concatenate([wide(k[0]) + wide(g) for k, g in zip(a, b)], axis=1)),
        keeps, gots,
    )
    for mask in wires.far[::-1]:
        last_got = swap(away, mask)
        if mask != wires.far[0]:
            mine, away = line.light(lambda a, b: cut(a + wide(b)), mine, line.take(last_got))
    out_done = line.light(lambda a, b: wide(a) + wide(b), out_keep[0], out_got)
    out_done = scatter_sum(wires, out_done, out_back[3:])
    out_away = line.light(low, out_done)
    out_got = wires.send(out_away, back_to)
    gu_back = line.light(return_rows, gu_half, flags=team_flags)
    gu_back[1:] = [swap(b, t) for b, t in zip(gu_back[1:], (one, two, one | two))]
    down_got = line.take(down_got)
    down_done = line.light(lambda a, b: low(a + wide(b)), down_mine, down_got)
    gu_back[1:], last_got, out_got, sums = line.take((gu_back[1:], last_got, out_got, sums))
    gu_sibling = swap_core(line.light(lambda *v: jnp.concatenate(v, axis=1), *gu_back))
    qkv_done = line.light(lambda a, b: low(a + wide(b)), mine, last_got)
    qkv_sibling = swap_core(qkv_done)
    out_low = line.light(lambda a, b: low(a + wide(b)), out_done, out_got)
    out_sibling = wires.send(
        out_low, lambda s, c: (s, 1 - c) if (s & top != 0) == (c == 1) else None
    )
    down_sibling = swap_core(down_done)
    sums_got = swap(sums, wires.masks[2])
    gu_sibling, qkv_sibling, out_sibling, down_sibling, sums_got = line.take(
        (gu_sibling, qkv_sibling, out_sibling, down_sibling, sums_got)
    )
    sums = sums + sums_got
    sums_got = swap(sums, wires.masks[3])
    gu_out = line.run(
        lambda *v: put_columns(
            list(v),
            FF // shards,
            team_blocks(wires, core) + [sum(team_blocks(wires, 1 - core), [])],
        ),
        *gu_back, gu_sibling,
    )
    down_out = line.run(
        lambda a, b: put_columns([a, b], half, [[core], [1 - core]]), down_done, down_sibling
    )
    qkv_out = line.run(
        lambda a, b: put_columns(
            [a, b], HEAD_SIZE, [sum(parcels(core), []), sum(parcels(1 - core), [])]
        ),
        qkv_done, qkv_sibling,
    )
    out_done = line.light(
        lambda home, a, b: wide(jnp.where(home, a, b)),
        out_low, out_sibling, flags=(at_home,),
    )
    sums = sums + line.take(sums_got)
    for mask in wires.masks[4:]:
        sums = sums + line.take(swap(sums, mask))
    lanes = d // HEAD_SIZE

    return (
        result,
        grad_tokens,
        sums[:lanes].reshape(-1),
        sums[2 * lanes],
        sums[2 * lanes + 1],
        sums[lanes : 2 * lanes].reshape(-1),
        qkv_out,
        out_done,
        gu_out,
        down_out,
    )


def solution(mesh):
    shards, copies = mesh.shape["shard"], mesh.shape["replica"]
    body = lambda *args: on_device(shards, copies, *args)
    in_specs = (
        P(("shard", "replica"), None),
        P(("shard", "replica"), None),
        P(),
        P(),
        P(),
        P(),
        P("shard", None),
        P("shard", None),
        P("shard", None),
        P("shard", None),
        P(("shard", "replica"), None),
    )
    out_specs = (
        P(("shard", "replica"), None),
        P(("shard", "replica"), None),
        P(),
        P(),
        P(),
        P(),
        P("shard", None),
        P("shard", None),
        P("shard", None),
        P("shard", None),
    )
    return jax.shard_map(
        body, mesh=mesh, in_specs=in_specs, out_specs=out_specs, check_vma=False
    )
```
